32 devices in a mesh: member: 2 (over y), gx: 4 (over z), gy: 4 (over x, core).
Axes of the slice: x: 2, y: 2, z: 4, core: 2. Of those that a mesh axis runs over, the one named last changes fastest.
Arguments:
- checkpoint: float32 [8, 4, 4, 12288], P(('member', 'gx'), 'gy'), parts along dimension 0, may hold values from -6 to 6
- holder_list: int32 [8, 4, 4], P(('member', 'gx'), 'gy'), parts along dimension 0, may hold values from 0 to 3, each once within a row
- height: float32 [64, 512], P(('member', 'gx'), 'gy'), parts along dimension 0, may hold values from -6 to 6
- land_mask: int32 [32, 512], P('gx', 'gy'), may hold values 0 or 1
- diffusivity: float32 [3, 16], replicated, may hold values from 0.02 to 0.2
- tracer_weight: float32 [6, 16, 32, 512], P('member', None, 'gx', 'gy'), parts along dimension 0, may hold values from -6 to 6
- height_weight: float32 [64, 512], P(('member', 'gx'), 'gy'), parts along dimension 0, may hold values from -6 to 6
Outputs:
- adjoint_tracers: float32 [6, 16, 32, 512], P('member', None, 'gx', 'gy'), parts along dimension 0
- adjoint_height: float32 [64, 512], P(('member', 'gx'), 'gy'), parts along dimension 0
The draws below stay inside these ranges and needn't reach their ends.
There are 2 independent parts, one for each index of `member`. The reference program is written for one: setup_inputs(seed, part) draws one part's arguments, and reference() takes and returns one part's arrays. A program takes and returns all parts, laid end to end along the dimension named above; an argument that names none is the same for every part. Nothing has to cross between parts.
Inputs may be any that keep to these rules, and one draw needn't show every extreme that they name: For each owner device (o, g), holder_list[o, g, :] names every longitude index once: each device along gx holds exactly one piece of every owner's tracers in its row.
All inputs are finite; a program needn't handle non-finite values. No bound on the sum of `land_mask` on one device may be relied on, other than what follows from the above.
Results may differ from the reference program's by a relative error of at most 0.0001.
Values sent between devices are 32-bit elements; how exact they have to be, the bound alone decides.
A program may use at most 64 MiB of HBM per device.

```python
import math
import jax
import jax.numpy as jnp
from jax import lax

CX = 8
CY = 128
LEV = 16
ITERS = 4
NX = 32
NY = 512
PIECE = 12288
N_GX = 4
N_GY = 4


def plant(drawn, key, low, top_value):
    extent = drawn.shape
    place = [jax.random.randint(jax.random.fold_in(key, axis), (), 0, extent[axis]) for axis in range(len(extent))]
    drawn = drawn.at[tuple(place)].set(low)
    longest = extent.index(max(extent))
    place[longest] = (place[longest] + 1) % extent[longest]
    return drawn.at[tuple(place)].set(top_value)


def steps_of(stream_key, dims, shards, least, high):
    loudness = 1.0
    for position, parts in shards:
        steps = jax.random.uniform(jax.random.fold_in(jax.random.fold_in(stream_key, 6), position), (parts,), jnp.float32, least / len(shards), high / len(shards))
        loudness = loudness * jnp.repeat(jnp.exp(steps), dims[position] // parts).reshape((-1,) + (1,) * (len(dims) - 1 - position))
    return loudness


def normal_values(rng, extent, deviation, reach, shards=(), dtype=jnp.bfloat16):
    drawn = deviation * jax.random.normal(rng, extent, jnp.float32)
    if shards:
        drawn = drawn * steps_of(rng, extent, shards, -0.22, 0.18)
    return jnp.clip(drawn, -reach, reach).astype(dtype)


def setup_inputs(seed: int = 0, part: int = 0) -> dict:
    key_of = jax.random.split(jax.random.key(seed), 8)
    part_splits = jax.random.split(jax.random.fold_in(key_of[7], part), 8)
    checkpoint = normal_values(part_splits[0], (N_GX, N_GY, N_GX, PIECE), 1.0, 6.0, ((0, 4), (1, 4)), jnp.float32)
    holder_list = jax.vmap(lambda own: jax.random.permutation(own, N_GX))(jax.random.split(part_splits[1], N_GX * N_GY)).reshape((N_GX, N_GY, N_GX)).astype(jnp.int32)
    height = normal_values(part_splits[2], (NX, NY), 1.0, 6.0, ((0, 4), (1, 4)), jnp.float32)
    land_mask = plant((jax.random.randint(key_of[3], (NX, NY), 0, 4) < 3).astype(jnp.int32), jax.random.fold_in(key_of[3], 1), 0, 1)
    diffusivity = jnp.clip(jnp.exp(jax.random.uniform(key_of[4], (3, LEV), jnp.float32, math.log(0.02), math.log(0.2))), 0.02, 0.2)
    tracer_weight = normal_values(part_splits[5], (3, LEV, NX, NY), 1.0, 6.0, ((2, 4), (3, 4)), jnp.float32)
    height_weight = normal_values(part_splits[6], (NX, NY), 1.0, 6.0, ((0, 4), (1, 4)), jnp.float32)
    return dict(checkpoint=checkpoint, holder_list=holder_list, height=height, land_mask=land_mask, diffusivity=diffusivity, tracer_weight=tracer_weight, height_weight=height_weight)


ADVECTION = 0.3
VERTICAL_MIX = 0.1
HEIGHT_DIFFUSION = 0.2
HEIGHT_DAMPING = 0.3
BUOYANCY = 0.5

def pad_field(field):
    field = jnp.concatenate([field[..., -1:, :], field, field[..., :1, :]], axis=-2)
    widths = [(0, 0)] * (field.ndim - 1) + [(1, 1)]
    return jnp.pad(field, widths)

def advance(height_pad, tracer_pad, wet_cells, diffusivity):
    east_cell = tracer_pad[..., 2:, 1:-1]
    west_cell = tracer_pad[..., :-2, 1:-1]
    north_cell = tracer_pad[..., 1:-1, 2:]
    south_cell = tracer_pad[..., 1:-1, :-2]
    centre = tracer_pad[..., 1:-1, 1:-1]
    height_mid = height_pad[1:-1, 1:-1]
    zonal = -0.5 * (height_pad[1:-1, 2:] - height_pad[1:-1, :-2])
    meridional = 0.5 * (height_pad[2:, 1:-1] - height_pad[:-2, 1:-1])
    advect = zonal * 0.5 * (east_cell - west_cell) + meridional * 0.5 * (north_cell - south_cell)
    laplace = east_cell + west_cell + north_cell + south_cell - 4.0 * centre
    upper = jnp.concatenate([centre[:, :1], centre[:, :-1]], axis=1)
    lower = jnp.concatenate([centre[:, 1:], centre[:, -1:]], axis=1)
    vertical = upper + lower - 2.0 * centre
    tracer_new = centre + wet_cells * (-ADVECTION * advect + diffusivity[:, :, None, None] * laplace + VERTICAL_MIX * vertical)
    height_lap = height_pad[2:, 1:-1] + height_pad[:-2, 1:-1] + height_pad[1:-1, 2:] + height_pad[1:-1, :-2] - 4.0 * height_mid
    height_new = height_mid + HEIGHT_DIFFUSION * height_lap - HEIGHT_DAMPING * jnp.tanh(height_mid) + BUOYANCY * wet_cells * lax.optimization_barrier(jnp.mean(centre[0], axis=0))
    return (height_new, tracer_new)

def reference(checkpoint, holder_list, height, land_mask, diffusivity, tracer_weight, height_weight):
    by_owner = jnp.transpose(checkpoint, (2, 1, 0, 3))
    pieces = jnp.take_along_axis(by_owner, holder_list[..., None].astype(jnp.int32), axis=2)
    pieces = pieces.reshape(N_GX, N_GY, 3, LEV, CX, CY)
    tracers = jnp.transpose(pieces, (2, 3, 0, 4, 1, 5)).reshape(3, LEV, NX, NY)
    wet_cells = land_mask.astype(jnp.float32)

    def forward(tracer_start, height_start):
        tracer_now, height_now = (tracer_start, height_start)
        for repeat in range(ITERS):
            height_now, tracer_now = advance(pad_field(height_now), pad_field(tracer_now), wet_cells, diffusivity)
        return (tracer_now, height_now)
    outputs, pullback = jax.vjp(forward, tracers, height)
    adjoint_tracers, adjoint_height = pullback((tracer_weight, height_weight))
    return (adjoint_tracers, adjoint_height)
```

```python
import functools
import jax
import jax.numpy as jnp
from jax import lax
from jax.experimental import pallas as pl
from jax.experimental.pallas import tpu as pltpu
from jax.sharding import PartitionSpec as P

ITERS = 4
ADVECTION = 0.3
VERTICAL_MIX = 0.1
HEIGHT_DIFFUSION = 0.2
HEIGHT_DAMPING = 0.3
BUOYANCY = 0.5

SUB = 8
LANE = 128
HALO = 4
GROUP = 16
GROUPS = LANE // GROUP
MESH = pl.DeviceIdType.MESH


def roll_lanes(value, shift):
    return pltpu.roll(value, shift, 1)


def roll_rows(value, shift):
    return pltpu.roll(value, shift, 0)


def kernel(
    n, n_y, levels, piece_rows,
    holder_hbm, diff_hbm, ckpt_hbm, height_hbm, mask_hbm, tw_hbm, hw_hbm,
    out_ref, outh_ref,
    buf, recv, state, strip, lam, slam, mu, smu, dy, sdy, pairs, sdiff,
    hf, af, bf, wf, lh, gu, gv, prow,
    em, es, el, zq, zl, xs, xr, ys, yr,
    holder_ref, diff_ref, ckpt_ref, height_ref, mask_ref, hw_ref,
    a2a_send, a2a_recv, send_sem, recv_sem, in_sem,
):
    me = lax.axis_index("gx")
    my = lax.axis_index("gy")
    east, west = lax.rem(me + 1, n), lax.rem(me + n - 1, n)
    north, south = lax.rem(my + 1, n_y), lax.rem(my + n_y - 1, n_y)
    channels = 3 * levels
    each = channels // GROUPS
    padded = -(-piece_rows // SUB) * SUB
    own = slice(SUB, 2 * SUB)
    blocks = (HALO, HALO + SUB)

    inputs = (
        (ckpt_hbm, ckpt_ref), (diff_hbm, diff_ref), (mask_hbm, mask_ref), (tw_hbm, lam.at[:, pl.ds(SUB, SUB)]),
        (height_hbm, height_ref), (hw_hbm, hw_ref), (holder_hbm, holder_ref),
    )
    loads = [pltpu.make_async_copy(source, target, in_sem.at[i]) for i, (source, target) in enumerate(inputs)]
    for load in loads:
        load.start()

    barrier = pltpu.get_barrier_semaphore()
    for k in range(1, n):
        pl.semaphore_signal(barrier, inc=1, device_id={"gx": lax.rem(me + k, n)}, device_id_type=MESH)
    for other in (north, south):
        pl.semaphore_signal(barrier, inc=1, device_id={"gy": other}, device_id_type=MESH)
        for side in (east, west):
            pl.semaphore_signal(barrier, inc=1, device_id={"gx": side, "gy": other}, device_id_type=MESH)

    loads[0].wait()
    if padded != piece_rows:
        buf[...] = jnp.zeros_like(buf)
    for o in range(0, n, SUB):
        size = min(SUB, n - o)
        for r in range(piece_rows):
            buf[pl.ds(o * padded + r, size, stride=padded), :] = ckpt_ref[o:o + size, r * LANE:(r + 1) * LANE]

    pl.semaphore_wait(barrier, n + 5)

    mine = pl.multiple_of(me * padded, SUB)
    sends = []
    a2a = []
    for k in range(1, n):
        owner = lax.rem(me + k, n)
        copy = pltpu.make_async_remote_copy(
            src_ref=buf.at[pl.ds(pl.multiple_of(owner * padded, SUB), padded)],
            dst_ref=recv.at[me],
            send_sem=a2a_send.at[k], recv_sem=a2a_recv.at[k],
            device_id={"gx": owner}, device_id_type=MESH,
        )
        copy.start()
        a2a.append(copy)
    recv[me] = buf[pl.ds(mine, padded), :]

    used = [0]

    def send(source, target, device):
        i = used[0]
        used[0] += 1
        copy = pltpu.make_async_remote_copy(
            src_ref=source, dst_ref=target, send_sem=send_sem.at[i], recv_sem=recv_sem.at[i],
            device_id=device, device_id_type=MESH,
        )
        copy.start()
        sends.append(copy)
        return copy

    def wait_all(copies):
        for copy in copies:
            copy.wait_recv()

    lane = lax.broadcasted_iota(jnp.int32, (SUB, LANE), 1)
    sub = lax.broadcasted_iota(jnp.int32, (SUB, LANE), 0)
    first_lane, last_lane = lane == 0, lane == LANE - 1
    group = lax.shift_right_logical(lane, 4)
    place = lane & (GROUP - 1)
    low, high = place < HALO, place >= GROUP - HALO
    half = place < GROUP // 2
    edge = place == HALO - 1
    below, above = jnp.where(low, my, 1), jnp.where(high, n_y - 1 - my, 1)
    inside = (below > 0) & (above > 0)
    zero = jnp.zeros((SUB, LANE), jnp.float32)

    def back(value, shift):
        return roll_lanes(value, (LANE - shift) % LANE)

    def everywhere(value):
        moved = [value] + [roll_lanes(value, GROUP * k) for k in range(1, GROUPS)]
        while len(moved) > 1:
            moved = [a + b for a, b in zip(moved[::2], moved[1::2])]
        return moved[0]

    def edges(from_south, from_north):
        return jnp.where(edge, from_south, back(from_north, GROUP - 2 * HALO + 2))

    def side_of(pair, g):
        return back(pair, g * GROUP + HALO - 1)

    def channel_of(s):
        return group * each + s

    def first_level(s):
        return (channel_of(s) & (levels - 1)) == 0

    def last_level(s):
        return (channel_of(s) & (levels - 1)) == levels - 1

    def level_up(c):
        return c - lax.div(lax.rem(c, levels) + (levels - 1), levels)

    def level_down(c):
        return c + lax.div(2 * (levels - 1) - lax.rem(c, levels), levels)

    def over(body, carry=0):
        return lax.fori_loop(0, each, body, carry, unroll=2)

    def pack_field(value):
        south_part = (lane >= HALO) & (lane < 2 * HALO)
        north_part = (lane >= 2 * HALO) & (lane < 3 * HALO)
        picked = jnp.where(south_part, roll_lanes(value, HALO), jnp.where(north_part, roll_lanes(value, 3 * HALO), 0.0))
        return everywhere(picked)

    def pack_strip(ref, s, rows):
        packed = zero
        for g in range(GROUPS):
            moved = roll_lanes(ref[g * each + s, rows, :], (g * GROUP + 2 * HALO) % LANE)
            packed = jnp.where(group == g, moved, packed)
        return packed

    def send_strips(which, ref):
        def body(q, carry):
            a, b = pack_strip(ref, 2 * q, own), pack_strip(ref, 2 * q + 1, own)
            zq[which, q] = jnp.where(half, back(a, HALO), roll_lanes(b, HALO))
            return carry

        lax.fori_loop(0, each // 2, body, 0, unroll=True)
        whole = zq.at[which]
        copies = []
        for side, other in enumerate((north, south)):
            for start, device in (
                (SUB, {"gy": other}), (0, {"gx": east, "gy": other}), (2 * SUB, {"gx": west, "gy": other}),
            ):
                copies.append(send(whole, zl.at[which, side, :, pl.ds(start, SUB)], device))
        return copies

    def build_strips(which, ref, put):
        def body(q, carry):
            for g in blocks:
                rows = slice(g, g + SUB)
                south_pair, north_pair = zl[which, 0, q, rows, :], zl[which, 1, q, rows, :]
                for k, (from_south, from_north) in enumerate((
                    (south_pair, roll_lanes(north_pair, GROUP // 2)), (back(south_pair, GROUP // 2), north_pair),
                )):
                    packed = pack_strip(ref, 2 * q + k, rows)
                    mid = jnp.where(half, back(packed, HALO), roll_lanes(packed, HALO))
                    value = jnp.where(low, from_south, jnp.where(high, from_north, mid))
                    put(2 * q + k, rows, jnp.where(inside, value, 0.0))
            return carry

        lax.fori_loop(0, each // 2, body, 0)

    def send_rows(ref, out, into, width, to_east, to_west):
        count = channels * width // SUB
        place_of = lax.div(sub, width)
        for side, start in enumerate((to_east, to_west)):
            def body(k, carry):
                value = zero
                for j in range(SUB // width):
                    rows = slice(start - width * j, start - width * j + SUB)
                    value = jnp.where(place_of == j, ref[k + j * count, rows, :], value)
                out[side, k] = value
                return carry

            lax.fori_loop(0, count, body, 0, unroll=4)
        return [send(out.at[0], into.at[0], {"gx": east}), send(out.at[1], into.at[1], {"gx": west})]

    def take_rows(ref, into, width, from_west, from_east):
        count = channels * width // SUB

        def body(k, carry):
            for side, (base, offset) in enumerate(((0, from_west), (2 * SUB, from_east - 2 * SUB))):
                value = into[side, k]
                rows = slice(base, base + SUB)
                mask = (sub >= offset) & (sub < offset + width)
                for j in range(SUB // width):
                    shift = (offset - width * j) % SUB
                    c = k + j * count
                    ref[c, rows, :] = jnp.where(mask, roll_rows(value, shift) if shift else value, ref[c, rows, :])
            return carry

        lax.fori_loop(0, count, body, 0, unroll=4)

    def send_fields(first, values):
        for k, value in enumerate(values):
            em[first + k, own, :] = value
            es[first + k] = pack_field(value)
        which = pl.ds(first, len(values))
        mid, before, after = pl.ds(SUB, SUB), pl.ds(0, SUB), pl.ds(2 * SUB, SUB)
        copies = [
            send(em.at[which, mid], em.at[which, before], {"gx": east}),
            send(em.at[which, mid], em.at[which, after], {"gx": west}),
        ]
        for side, other in enumerate((north, south)):
            copies.append(send(es.at[which], el.at[side, which, mid], {"gy": other}))
            copies.append(send(es.at[which], el.at[side, which, before], {"gx": east, "gy": other}))
            copies.append(send(es.at[which], el.at[side, which, after], {"gx": west, "gy": other}))
        return copies

    def take_field(k, target):
        for r in range(0, 3 * SUB, SUB):
            rows = slice(r, r + SUB)
            value = em[k, rows, :]
            piece = jnp.where(
                low, back(el[0, k, rows, :], GROUP // 2),
                jnp.where(high, roll_lanes(el[1, k, rows, :], GROUP // 2), pack_field(value)),
            )
            target[0, rows, :] = value
            target[1, rows, :] = jnp.where(inside, piece, 0.0)

    def along(field, g, shift):
        return field[0, g + shift:g + shift + SUB, :], field[1, g + shift:g + shift + SUB, :]

    def latitude(main, piece):
        side = side_of(edges(piece, piece), 0)
        h_n = jnp.where(last_lane, side, back(main, 1))
        h_s = jnp.where(first_lane, side, roll_lanes(main, 1))
        return h_n, h_s, back(piece, 1), roll_lanes(piece, 1)

    def total_of(step, rows):
        main = state[step, 0, rows, :]
        for c in range(1, levels):
            main = main + state[step, c, rows, :]
        piece = zero
        for s in range(each):
            piece = piece + jnp.where(channel_of(s) < levels, strip[step, s + 1, rows, :], 0.0)
        return main, everywhere(piece)

    def slopes(step, advance):
        for g in blocks:
            rows = slice(g, g + SUB)
            main, piece = along(hf.at[step], g, 0)
            main_e, piece_e = along(hf.at[step], g, 1)
            main_w, piece_w = along(hf.at[step], g, -1)
            main_n, main_s, piece_n, piece_s = latitude(main, piece)
            af[step, 0, rows, :] = (-0.25 * ADVECTION) * (main_n - main_s)
            af[step, 1, rows, :] = (-0.25 * ADVECTION) * (piece_n - piece_s)
            bf[step, 0, rows, :] = (0.25 * ADVECTION) * (main_e - main_w)
            bf[step, 1, rows, :] = (0.25 * ADVECTION) * (piece_e - piece_w)
            if not advance:
                continue
            totals = total_of(step, rows)
            for k, (h, h_e, h_w, h_n, h_s) in enumerate((
                (main, main_e, main_w, main_n, main_s), (piece, piece_e, piece_w, piece_n, piece_s),
            )):
                lap = h_e + h_w + h_n + h_s - 4.0 * h
                value = h + HEIGHT_DIFFUSION * lap - HEIGHT_DAMPING * jnp.tanh(h)
                value = value + (BUOYANCY / levels) * wf[k, rows, :] * totals[k]
                hf[step + 1, k, rows, :] = jnp.where(inside, value, 0.0) if k else value

    def wrap_strips(ref):
        for g in blocks:
            rows = slice(g, g + SUB)
            ref[0, rows, :] = roll_lanes(ref[each, rows, :], GROUP)
            ref[each + 1, rows, :] = back(ref[1, rows, :], GROUP)

    def strip_vertical(ref, s, rows, value):
        upper = jnp.where(first_level(s), value, ref[s, rows, :])
        lower = jnp.where(last_level(s), value, ref[s + 2, rows, :])
        return upper + lower - 2.0 * value

    for load in loads[1:]:
        load.wait()
    fields_a = send_fields(0, (height_ref[...], mask_ref[...].astype(jnp.float32), hw_ref[...]))

    for s in range(each):
        value = zero
        for g in range(GROUPS):
            c = g * each + s
            value = jnp.where(group == g, diff_ref[c // levels, c % levels], value)
        sdiff[s] = value
    for step in range(1, ITERS):
        for k in range(2):
            hf[step, k, 0:SUB, :] = zero
            hf[step, k, 2 * SUB:3 * SUB, :] = zero
    for k in range(2):
        for r in range(0, 3 * SUB, SUB):
            gu[k, r:r + SUB, :] = zero
            gv[k, r:r + SUB, :] = zero

    for copy in a2a:
        copy.wait_recv()
    first = state.at[0]
    for p in range(n):
        holder = holder_ref[0, 0, p]
        if piece_rows % SUB == 0:
            depth = piece_rows // SUB
            for c in range(depth):
                first[p * depth + c, own, :] = recv[holder, c * SUB:(c + 1) * SUB, :]
        else:
            for r in range(piece_rows):
                row = p * piece_rows + r
                at = SUB + row % SUB
                first[row // SUB, at:at + 1, :] = recv[holder, r:r + 1, :]

    start_copies = send_rows(first, xs.at[0], xr.at[0], HALO, 3 * HALO, 2 * HALO)
    start_copies += send_strips(0, first)
    weight_copies = send_rows(lam, xs.at[1], xr.at[1], HALO, 3 * HALO, 2 * HALO)
    weight_copies += send_strips(1, lam)

    wait_all(fields_a)
    take_field(0, hf.at[0])
    take_field(1, wf)
    take_field(2, lh)

    def put_first(s, rows, value):
        strip[0, s + 1, rows, :] = value
        pairs[s, rows, :] = edges(value, value)

    wait_all(start_copies)
    take_rows(first, xr.at[0], HALO, HALO, 2 * SUB)
    build_strips(0, first, put_first)
    wrap_strips(strip.at[0])

    def forward(step):
        def body(s, carry):
            for r in blocks:
                rows, rows_e, rows_w = (slice(r + d, r + d + SUB) for d in (0, 1, -1))
                pair = pairs[s, rows, :]
                a, b, w = af[step, 0, rows, :], bf[step, 0, rows, :], wf[0, rows, :]
                for g in range(GROUPS):
                    c = g * each + s
                    value = state[step, c, rows, :]
                    side = side_of(pair, g)
                    c_s = jnp.where(first_lane, side, roll_lanes(value, 1))
                    c_n = jnp.where(last_lane, side, back(value, 1))
                    c_e, c_w = state[step, c, rows_e, :], state[step, c, rows_w, :]
                    vert = state[step, level_up(c), rows, :] + state[step, level_down(c), rows, :] - 2.0 * value
                    delta = c_n - c_s
                    if step < 2:
                        dy[step, c, rows, :] = delta
                    lap = c_e + c_w + c_n + c_s - 4.0 * value
                    d = diff_ref[lax.div(c, levels), lax.rem(c, levels)]
                    state[step + 1, c, rows, :] = value + w * (
                        d * lap - a * (c_e - c_w) - b * delta + VERTICAL_MIX * vert
                    )
                a, b, w = af[step, 1, rows, :], bf[step, 1, rows, :], wf[1, rows, :]
                value = strip[step, s + 1, rows, :]
                c_s, c_n = roll_lanes(value, 1), back(value, 1)
                c_e, c_w = strip[step, s + 1, rows_e, :], strip[step, s + 1, rows_w, :]
                delta = c_n - c_s
                if step < 2:
                    sdy[step, s, rows, :] = delta
                lap = c_e + c_w + c_n + c_s - 4.0 * value
                vert = strip_vertical(strip.at[step], s, rows, value)
                value = value + w * (sdiff[s] * lap - a * (c_e - c_w) - b * delta + VERTICAL_MIX * vert)
                strip[step + 1, s + 1, rows, :] = value
                pairs[s, rows, :] = edges(value, value)
            return carry

        over(body)

    outer_copies, fields_b = [], []
    for step in range(ITERS - 1):
        slopes(step, True)
        if step == 1:
            fields_b = send_fields(3, (hf[2, 0, own, :],))
        forward(step)
        if step == 1:
            outer_copies = send_rows(state.at[2], ys, yr, 2, 3 * HALO, 2 * HALO + 2)
            outer_copies += send_strips(2, state.at[2])
        if step < 2:
            wrap_strips(strip.at[step + 1])
    slopes(3, False)

    def last_sums(s, carry):
        total_u, total_v = carry
        pair = pairs[s, own, :]
        for g in range(GROUPS):
            c = g * each + s
            value = state[3, c, own, :]
            side = side_of(pair, g)
            m = wf[0, own, :] * lam[c, own, :]
            delta = jnp.where(last_lane, side, back(value, 1)) - jnp.where(first_lane, side, roll_lanes(value, 1))
            total_u = total_u + m * (state[3, c, SUB + 1:2 * SUB + 1, :] - state[3, c, SUB - 1:2 * SUB - 1, :])
            total_v = total_v + m * delta
        return total_u, total_v

    total_u, total_v = over(last_sums, (zero, zero))
    fields_c = send_fields(4, (total_u, total_v, hf[3, 0, own, :], af[3, 0, own, :]))

    def put_weight(s, rows, value):
        slam[s, rows, :] = value

    wait_all(weight_copies)
    take_rows(lam, xr.at[1], HALO, HALO, 2 * SUB)
    build_strips(1, lam, put_weight)

    def spread_pair(step, s, rows, m):
        bm = bf[step, 1, rows, :] * m
        dm = sdiff[s] * m
        pairs[s, rows, :] = edges(dm - bm, dm + bm)

    def put_outer(s, rows, value):
        sdy[2, s, rows, :] = back(value, 1) - roll_lanes(value, 1)
        strip[2, s + 1, rows, :] = value
        pairs[s, rows, :] = edges(value, value)

    wait_all(outer_copies)
    take_rows(state.at[2], yr, 2, HALO, 2 * SUB + 2)
    build_strips(2, state.at[2], put_outer)

    def outer_slopes(s, carry):
        for r in blocks:
            rows = slice(r, r + SUB)
            pair = pairs[s, rows, :]
            for g in range(GROUPS):
                c = g * each + s
                value = state[2, c, rows, :]
                side = side_of(pair, g)
                dy[2, c, rows, :] = (
                    jnp.where(last_lane, side, back(value, 1)) - jnp.where(first_lane, side, roll_lanes(value, 1))
                )
        return carry

    over(outer_slopes)
    wait_all(fields_b)
    take_field(3, hf.at[2])
    slopes(2, False)
    wait_all(fields_c)
    take_field(4, gu)
    take_field(5, gv)
    take_field(6, hf.at[3])
    slopes(3, False)
    take_field(7, af.at[3])
    for copy in a2a + sends:
        copy.wait_send()

    def weigh(s, carry):
        for r in blocks:
            rows = slice(r, r + SUB)
            for g in range(GROUPS):
                c = g * each + s
                mu[c, rows, :] = wf[0, rows, :] * lam[c, rows, :]
            m = wf[1, rows, :] * slam[s, rows, :]
            smu[s + 1, rows, :] = m
            spread_pair(3, s, rows, m)
        return carry

    def sums(step):
        def body(s, carry):
            result = []
            for r, (total_u, total_v, strip_u, strip_v) in zip(blocks, (carry[:4], carry[4:])):
                rows, rows_e, rows_w = (slice(r + d, r + d + SUB) for d in (0, 1, -1))
                w = wf[0, rows, :]
                for g in range(GROUPS):
                    c = g * each + s
                    m = w * lam[c, rows, :]
                    mu[c, rows, :] = m
                    total_u = total_u + m * (state[step, c, rows_e, :] - state[step, c, rows_w, :])
                    total_v = total_v + m * dy[step, c, rows, :]
                m = wf[1, rows, :] * slam[s, rows, :]
                smu[s + 1, rows, :] = m
                strip_u = strip_u + m * (strip[step, s + 1, rows_e, :] - strip[step, s + 1, rows_w, :])
                strip_v = strip_v + m * sdy[step, s, rows, :]
                spread_pair(step, s, rows, m)
                result += [total_u, total_v, strip_u, strip_v]
            return tuple(result)

        totals = over(body, (zero,) * 8)
        for r, (total_u, total_v, strip_u, strip_v) in zip(blocks, (totals[:4], totals[4:])):
            rows = slice(r, r + SUB)
            gu[0, rows, :], gv[0, rows, :] = total_u, total_v
            gu[1, rows, :], gv[1, rows, :] = everywhere(strip_u), everywhere(strip_v)

    def adjoint(step):
        last = step == 0

        def body(s, carry):
            for r in (SUB,) if last else blocks:
                rows, rows_e, rows_w = (slice(r + d, r + d + SUB) for d in (0, 1, -1))
                pair = pairs[s, rows, :]
                a_e, a_w, b = af[step, 0, rows_e, :], af[step, 0, rows_w, :], bf[step, 0, rows, :]
                push = prow[0, rows, :]
                for g in range(GROUPS):
                    c = g * each + s
                    m = mu[c, rows, :]
                    m_e, m_w = mu[c, rows_e, :], mu[c, rows_w, :]
                    vert = mu[level_up(c), rows, :] + mu[level_down(c), rows, :] - 2.0 * m
                    d = diff_ref[lax.div(c, levels), lax.rem(c, levels)]
                    bm = b * m
                    dm = d * m
                    side = side_of(pair, g)
                    from_s = jnp.where(first_lane, side, roll_lanes(dm - bm, 1))
                    from_n = jnp.where(last_lane, side, back(dm + bm, 1))
                    value = lam[c, rows, :] + VERTICAL_MIX * vert - 4.0 * dm + from_s + from_n
                    value = value + d * (m_w + m_e) + (a_e * m_e - a_w * m_w)
                    if (g + 1) * each <= levels:
                        value = value + push
                    elif g * each < levels:
                        value = value + jnp.where(c < levels, 1.0, 0.0) * push
                    if last:
                        out_ref[c] = value
                    else:
                        lam[c, rows, :] = value
                if last:
                    continue
                m, m_e, m_w = smu[s + 1, rows, :], smu[s + 1, rows_e, :], smu[s + 1, rows_w, :]
                bm = bf[step, 1, rows, :] * m
                dm = sdiff[s] * m
                value = slam[s, rows, :] + VERTICAL_MIX * strip_vertical(smu, s, rows, m) - 4.0 * dm
                value = value + roll_lanes(dm - bm, 1) + back(dm + bm, 1) + sdiff[s] * (m_w + m_e)
                value = value + (af[step, 1, rows_e, :] * m_e - af[step, 1, rows_w, :] * m_w)
                slam[s, rows, :] = value + jnp.where(channel_of(s) < levels, prow[1, rows, :], 0.0)
            return carry

        over(body)

    for step in reversed(range(ITERS)):
        if step == ITERS - 1:
            over(weigh)
        else:
            sums(step)
        wrap_strips(smu)
        results = []
        for g in blocks:
            rows = slice(g, g + SUB)
            parts = []
            for k in range(2):
                value = lh[k, rows, :]
                prow[k, rows, :] = (BUOYANCY / levels) * wf[k, rows, :] * value
                turn = (0.25 * ADVECTION) * gu[k, rows, :]
                spread = HEIGHT_DIFFUSION * value
                damp = jnp.tanh(hf[step, k, rows, :])
                kept = value - 4.0 * spread - HEIGHT_DAMPING * (1.0 - damp * damp) * value
                before, after = slice(g - 1, g - 1 + SUB), slice(g + 1, g + 1 + SUB)
                kept = kept + HEIGHT_DIFFUSION * (lh[k, before, :] + lh[k, after, :])
                kept = kept + (0.25 * ADVECTION) * (gv[k, after, :] - gv[k, before, :])
                parts.append((kept, spread + turn, spread - turn))
            (main, to_n, to_s), (piece, piece_n, piece_s) = parts
            side = side_of(edges(piece_n, piece_s), 0)
            main = main + jnp.where(first_lane, side, roll_lanes(to_n, 1)) + jnp.where(last_lane, side, back(to_s, 1))
            piece = piece + roll_lanes(piece_n, 1) + back(piece_s, 1)
            results.append((main, jnp.where(inside, piece, 0.0)))
        for g, result in zip(blocks, results):
            for k in range(2):
                lh[k, g:g + SUB, :] = result[k]
        adjoint(step)

    outh_ref[...] = lh[0, own, :]


def local(checkpoint, holder_list, height, land_mask, diffusivity, tracer_weight, height_weight):
    n, n_y = lax.axis_size("gx"), lax.axis_size("gy")
    width_x, width_y = height.shape
    assert (width_x, width_y) == (SUB, LANE)
    levels = diffusivity.shape[1]
    channels = 3 * levels
    each = channels // GROUPS
    piece_rows = checkpoint.shape[3] // LANE
    padded = -(-piece_rows // SUB) * SUB
    f32 = jnp.float32
    vmem = pl.BlockSpec(memory_space=pltpu.VMEM)
    tile = pltpu.VMEM((SUB, LANE), f32)
    field = pltpu.VMEM((2, 3 * SUB, LANE), f32)
    fields = pltpu.VMEM((ITERS, 2, 3 * SUB, LANE), f32)
    volume = pltpu.VMEM((channels, 3 * SUB, LANE), f32)

    def strips(*lead):
        return pltpu.VMEM((*lead, 3 * SUB, LANE), f32)

    half = channels * HALO // SUB
    out, out_h = pl.pallas_call(
        functools.partial(kernel, n, n_y, levels, piece_rows),
        out_shape=(
            jax.ShapeDtypeStruct((channels, SUB, LANE), f32),
            jax.ShapeDtypeStruct((SUB, LANE), f32),
        ),
        in_specs=[pl.BlockSpec(memory_space=pltpu.HBM)] * 7,
        out_specs=(vmem, vmem),
        scratch_shapes=[
            pltpu.VMEM((n * padded, LANE), f32),
            pltpu.VMEM((n, padded, LANE), f32),
            pltpu.VMEM((ITERS, channels, 3 * SUB, LANE), f32),
            strips(ITERS, each + 2),
            volume, strips(each),
            volume, strips(each + 2),
            pltpu.VMEM((3, channels, 3 * SUB, LANE), f32), strips(3, each),
            strips(each),
            pltpu.VMEM((each, SUB, LANE), f32),
            fields, fields, fields,
            field, field, field, field, field,
            strips(8),
            pltpu.VMEM((8, SUB, LANE), f32),
            strips(2, 8),
            pltpu.VMEM((3, each // 2, SUB, LANE), f32),
            strips(3, 2, each // 2),
            pltpu.VMEM((2, 2, half, SUB, LANE), f32),
            pltpu.VMEM((2, 2, half, SUB, LANE), f32),
            pltpu.VMEM((2, half // 2, SUB, LANE), f32),
            pltpu.VMEM((2, half // 2, SUB, LANE), f32),
            pltpu.SMEM(holder_list.shape, jnp.int32),
            pltpu.SMEM(diffusivity.shape, f32),
            pltpu.VMEM(checkpoint.shape[2:], f32),
            tile,
            pltpu.VMEM((SUB, LANE), jnp.int32),
            tile,
            pltpu.SemaphoreType.DMA((n,)),
            pltpu.SemaphoreType.DMA((n,)),
            pltpu.SemaphoreType.DMA((48,)),
            pltpu.SemaphoreType.DMA((48,)),
            pltpu.SemaphoreType.DMA((7,)),
        ],
        compiler_params=pltpu.CompilerParams(
            collective_id=0, has_side_effects=True, vmem_limit_bytes=60 * 2**20
        ),
    )(
        holder_list, diffusivity, checkpoint.reshape(checkpoint.shape[2:]), height, land_mask,
        tracer_weight.reshape(channels, SUB, LANE), height_weight,
    )
    return out.reshape(tracer_weight.shape), out_h


def solution(mesh):
    return jax.shard_map(
        local,
        mesh=mesh,
        in_specs=(
            P(("member", "gx"), "gy", None, None),
            P(("member", "gx"), "gy", None),
            P(("member", "gx"), "gy"),
            P("gx", "gy"),
            P(),
            P("member", None, "gx", "gy"),
            P(("member", "gx"), "gy"),
        ),
        out_specs=(P("member", None, "gx", "gy"), P(("member", "gx"), "gy")),
        check_vma=False,
    )
```

```python
import functools
import jax
import jax.numpy as jnp
from jax import lax
from jax.experimental import pallas as pl
from jax.experimental.pallas import tpu as pltpu
from jax.sharding import PartitionSpec as P

ITERS = 4
ADVECTION = 0.3
VERTICAL_MIX = 0.1
HEIGHT_DIFFUSION = 0.2
HEIGHT_DAMPING = 0.3
BUOYANCY = 0.5

SUB = 8
LANE = 128
HALO = 4
GROUP = 16
GROUPS = LANE // GROUP
MESH = pl.DeviceIdType.MESH


def roll_lanes(value, shift):
    return pltpu.roll(value, shift, 1)


def roll_rows(value, shift):
    return pltpu.roll(value, shift, 0)


def kernel(
    n, n_y, levels, piece_rows,
    holder_hbm, diff_hbm, ckpt_hbm, height_hbm, mask_hbm, tw_hbm, hw_hbm,
    out_ref, outh_ref,
    buf, recv, state, strip, lam, slam, mu, smu, dy, sdy, pairs, sdiff,
    hf, af, bf, wf, lh, gu, gv, prow,
    em, es, el, zq, zl, xs, xr, ys, yr,
    holder_ref, diff_ref, ckpt_ref, height_ref, mask_ref, hw_ref,
    a2a_send, a2a_recv, send_sem, recv_sem, in_sem,
):
    me = lax.axis_index("gx")
    my = lax.axis_index("gy")
    east, west = lax.rem(me + 1, n), lax.rem(me + n - 1, n)
    north, south = lax.rem(my + 1, n_y), lax.rem(my + n_y - 1, n_y)
    channels = 3 * levels
    each = channels // GROUPS
    padded = -(-piece_rows // SUB) * SUB
    own = slice(SUB, 2 * SUB)
    blocks = (HALO, HALO + SUB)

    inputs = (
        (ckpt_hbm, ckpt_ref), (diff_hbm, diff_ref), (mask_hbm, mask_ref), (tw_hbm, lam.at[:, pl.ds(SUB, SUB)]),
        (height_hbm, height_ref), (hw_hbm, hw_ref), (holder_hbm, holder_ref),
    )
    loads = [pltpu.make_async_copy(source, target, in_sem.at[i]) for i, (source, target) in enumerate(inputs)]
    for load in loads:
        load.start()

    barrier = pltpu.get_barrier_semaphore()
    for k in range(1, n):
        pl.semaphore_signal(barrier, inc=1, device_id={"gx": lax.rem(me + k, n)}, device_id_type=MESH)
    for other in (north, south):
        pl.semaphore_signal(barrier, inc=1, device_id={"gy": other}, device_id_type=MESH)
        for side in (east, west):
            pl.semaphore_signal(barrier, inc=1, device_id={"gx": side, "gy": other}, device_id_type=MESH)

    loads[0].wait()
    if padded != piece_rows:
        buf[...] = jnp.zeros_like(buf)
    for o in range(0, n, SUB):
        size = min(SUB, n - o)
        for r in range(piece_rows):
            buf[pl.ds(o * padded + r, size, stride=padded), :] = ckpt_ref[o:o + size, r * LANE:(r + 1) * LANE]

    pl.semaphore_wait(barrier, n + 5)

    mine = pl.multiple_of(me * padded, SUB)
    sends = []
    a2a = []
    for k in range(1, n):
        owner = lax.rem(me + k, n)
        copy = pltpu.make_async_remote_copy(
            src_ref=buf.at[pl.ds(pl.multiple_of(owner * padded, SUB), padded)],
            dst_ref=recv.at[me],
            send_sem=a2a_send.at[k], recv_sem=a2a_recv.at[k],
            device_id={"gx": owner}, device_id_type=MESH,
        )
        copy.start()
        a2a.append(copy)
    recv[me] = buf[pl.ds(mine, padded), :]

    used = [0]

    def send(source, target, device):
        i = used[0]
        used[0] += 1
        copy = pltpu.make_async_remote_copy(
            src_ref=source, dst_ref=target, send_sem=send_sem.at[i], recv_sem=recv_sem.at[i],
            device_id=device, device_id_type=MESH,
        )
        copy.start()
        sends.append(copy)
        return copy

    def wait_all(copies):
        for copy in copies:
            copy.wait_recv()

    lane = lax.broadcasted_iota(jnp.int32, (SUB, LANE), 1)
    sub = lax.broadcasted_iota(jnp.int32, (SUB, LANE), 0)
    first_lane, last_lane = lane == 0, lane == LANE - 1
    group = lax.shift_right_logical(lane, 4)
    place = lane & (GROUP - 1)
    low, high = place < HALO, place >= GROUP - HALO
    half = place < GROUP // 2
    edge = place == HALO - 1
    below, above = jnp.where(low, my, 1), jnp.where(high, n_y - 1 - my, 1)
    inside = (below > 0) & (above > 0)
    zero = jnp.zeros((SUB, LANE), jnp.float32)

    def back(value, shift):
        return roll_lanes(value, (LANE - shift) % LANE)

    def everywhere(value):
        moved = [value] + [roll_lanes(value, GROUP * k) for k in range(1, GROUPS)]
        while len(moved) > 1:
            moved = [a + b for a, b in zip(moved[::2], moved[1::2])]
        return moved[0]

    def edges(from_south, from_north):
        return jnp.where(edge, from_south, back(from_north, GROUP - 2 * HALO + 2))

    def side_of(pair, g):
        return back(pair, g * GROUP + HALO - 1)

    def channel_of(s):
        return group * each + s

    def first_level(s):
        return (channel_of(s) & (levels - 1)) == 0

    def last_level(s):
        return (channel_of(s) & (levels - 1)) == levels - 1

    def level_up(c):
        return c - 1 if c % levels else c

    def level_down(c):
        return c + 1 if (c + 1) % levels else c

    def over(body, carry=0):
        for s in range(each):
            carry = body(s, carry)
        return carry

    def pack_field(value):
        south_part = (lane >= HALO) & (lane < 2 * HALO)
        north_part = (lane >= 2 * HALO) & (lane < 3 * HALO)
        picked = jnp.where(south_part, roll_lanes(value, HALO), jnp.where(north_part, roll_lanes(value, 3 * HALO), 0.0))
        return everywhere(picked)

    def pack_strip(ref, s, rows):
        packed = zero
        for g in range(GROUPS):
            moved = roll_lanes(ref[g * each + s, rows, :], (g * GROUP + 2 * HALO) % LANE)
            packed = jnp.where(group == g, moved, packed)
        return packed

    def send_strips(which, ref):
        def body(q, carry):
            a, b = pack_strip(ref, 2 * q, own), pack_strip(ref, 2 * q + 1, own)
            zq[which, q] = jnp.where(half, back(a, HALO), roll_lanes(b, HALO))
            return carry

        lax.fori_loop(0, each // 2, body, 0, unroll=True)
        whole = zq.at[which]
        copies = []
        for side, other in enumerate((north, south)):
            for start, device in (
                (SUB, {"gy": other}), (0, {"gx": east, "gy": other}), (2 * SUB, {"gx": west, "gy": other}),
            ):
                copies.append(send(whole, zl.at[which, side, :, pl.ds(start, SUB)], device))
        return copies

    def build_strips(which, ref, put):
        def body(q, carry):
            for g in blocks:
                rows = slice(g, g + SUB)
                south_pair, north_pair = zl[which, 0, q, rows, :], zl[which, 1, q, rows, :]
                for k, (from_south, from_north) in enumerate((
                    (south_pair, roll_lanes(north_pair, GROUP // 2)), (back(south_pair, GROUP // 2), north_pair),
                )):
                    packed = pack_strip(ref, 2 * q + k, rows)
                    mid = jnp.where(half, back(packed, HALO), roll_lanes(packed, HALO))
                    value = jnp.where(low, from_south, jnp.where(high, from_north, mid))
                    put(2 * q + k, rows, jnp.where(inside, value, 0.0))
            return carry

        lax.fori_loop(0, each // 2, body, 0)

    def send_rows(ref, out, into, width, to_east, to_west):
        count = channels * width // SUB
        place_of = lax.div(sub, width)
        for side, start in enumerate((to_east, to_west)):
            def body(k, carry):
                value = zero
                for j in range(SUB // width):
                    rows = slice(start - width * j, start - width * j + SUB)
                    value = jnp.where(place_of == j, ref[k + j * count, rows, :], value)
                out[side, k] = value
                return carry

            lax.fori_loop(0, count, body, 0, unroll=4)
        return [send(out.at[0], into.at[0], {"gx": east}), send(out.at[1], into.at[1], {"gx": west})]

    def take_rows(ref, into, width, from_west, from_east):
        count = channels * width // SUB

        def body(k, carry):
            for side, (base, offset) in enumerate(((0, from_west), (2 * SUB, from_east - 2 * SUB))):
                value = into[side, k]
                rows = slice(base, base + SUB)
                mask = (sub >= offset) & (sub < offset + width)
                for j in range(SUB // width):
                    shift = (offset - width * j) % SUB
                    c = k + j * count
                    ref[c, rows, :] = jnp.where(mask, roll_rows(value, shift) if shift else value, ref[c, rows, :])
            return carry

        lax.fori_loop(0, count, body, 0, unroll=4)

    def send_fields(first, values):
        for k, value in enumerate(values):
            em[first + k, own, :] = value
            es[first + k] = pack_field(value)
        which = pl.ds(first, len(values))
        mid, before, after = pl.ds(SUB, SUB), pl.ds(0, SUB), pl.ds(2 * SUB, SUB)
        copies = [
            send(em.at[which, mid], em.at[which, before], {"gx": east}),
            send(em.at[which, mid], em.at[which, after], {"gx": west}),
        ]
        for side, other in enumerate((north, south)):
            copies.append(send(es.at[which], el.at[side, which, mid], {"gy": other}))
            copies.append(send(es.at[which], el.at[side, which, before], {"gx": east, "gy": other}))
            copies.append(send(es.at[which], el.at[side, which, after], {"gx": west, "gy": other}))
        return copies

    def take_field(k, target):
        for r in range(0, 3 * SUB, SUB):
            rows = slice(r, r + SUB)
            value = em[k, rows, :]
            piece = jnp.where(
                low, back(el[0, k, rows, :], GROUP // 2),
                jnp.where(high, roll_lanes(el[1, k, rows, :], GROUP // 2), pack_field(value)),
            )
            target[0, rows, :] = value
            target[1, rows, :] = jnp.where(inside, piece, 0.0)

    def along(field, g, shift):
        return field[0, g + shift:g + shift + SUB, :], field[1, g + shift:g + shift + SUB, :]

    def latitude(main, piece):
        side = side_of(edges(piece, piece), 0)
        h_n = jnp.where(last_lane, side, back(main, 1))
        h_s = jnp.where(first_lane, side, roll_lanes(main, 1))
        return h_n, h_s, back(piece, 1), roll_lanes(piece, 1)

    def total_of(step, rows):
        main = state[step, 0, rows, :]
        for c in range(1, levels):
            main = main + state[step, c, rows, :]
        piece = zero
        for s in range(each):
            piece = piece + jnp.where(channel_of(s) < levels, strip[step, s + 1, rows, :], 0.0)
        return main, everywhere(piece)

    def slopes(step, advance):
        for g in blocks:
            rows = slice(g, g + SUB)
            main, piece = along(hf.at[step], g, 0)
            main_e, piece_e = along(hf.at[step], g, 1)
            main_w, piece_w = along(hf.at[step], g, -1)
            main_n, main_s, piece_n, piece_s = latitude(main, piece)
            af[step, 0, rows, :] = (-0.25 * ADVECTION) * (main_n - main_s)
            af[step, 1, rows, :] = (-0.25 * ADVECTION) * (piece_n - piece_s)
            bf[step, 0, rows, :] = (0.25 * ADVECTION) * (main_e - main_w)
            bf[step, 1, rows, :] = (0.25 * ADVECTION) * (piece_e - piece_w)
            if not advance:
                continue
            totals = total_of(step, rows)
            for k, (h, h_e, h_w, h_n, h_s) in enumerate((
                (main, main_e, main_w, main_n, main_s), (piece, piece_e, piece_w, piece_n, piece_s),
            )):
                lap = h_e + h_w + h_n + h_s - 4.0 * h
                value = h + HEIGHT_DIFFUSION * lap - HEIGHT_DAMPING * jnp.tanh(h)
                value = value + (BUOYANCY / levels) * wf[k, rows, :] * totals[k]
                hf[step + 1, k, rows, :] = jnp.where(inside, value, 0.0) if k else value

    def wrap_strips(ref):
        for g in blocks:
            rows = slice(g, g + SUB)
            ref[0, rows, :] = roll_lanes(ref[each, rows, :], GROUP)
            ref[each + 1, rows, :] = back(ref[1, rows, :], GROUP)

    def strip_vertical(ref, s, rows, value):
        upper = jnp.where(first_level(s), value, ref[s, rows, :])
        lower = jnp.where(last_level(s), value, ref[s + 2, rows, :])
        return upper + lower - 2.0 * value

    for load in loads[1:]:
        load.wait()
    fields_a = send_fields(0, (height_ref[...], mask_ref[...].astype(jnp.float32), hw_ref[...]))

    for s in range(each):
        value = zero
        for g in range(GROUPS):
            c = g * each + s
            value = jnp.where(group == g, diff_ref[c // levels, c % levels], value)
        sdiff[s] = value
    for step in range(1, ITERS):
        for k in range(2):
            hf[step, k, 0:SUB, :] = zero
            hf[step, k, 2 * SUB:3 * SUB, :] = zero
    for k in range(2):
        for r in range(0, 3 * SUB, SUB):
            gu[k, r:r + SUB, :] = zero
            gv[k, r:r + SUB, :] = zero

    for copy in a2a:
        copy.wait_recv()
    first = state.at[0]
    for p in range(n):
        holder = holder_ref[0, 0, p]
        if piece_rows % SUB == 0:
            depth = piece_rows // SUB
            for c in range(depth):
                first[p * depth + c, own, :] = recv[holder, c * SUB:(c + 1) * SUB, :]
        else:
            for r in range(piece_rows):
                row = p * piece_rows + r
                at = SUB + row % SUB
                first[row // SUB, at:at + 1, :] = recv[holder, r:r + 1, :]

    start_copies = send_rows(first, xs.at[0], xr.at[0], HALO, 3 * HALO, 2 * HALO)
    start_copies += send_strips(0, first)
    weight_copies = send_rows(lam, xs.at[1], xr.at[1], HALO, 3 * HALO, 2 * HALO)
    weight_copies += send_strips(1, lam)

    wait_all(fields_a)
    take_field(0, hf.at[0])
    take_field(1, wf)
    take_field(2, lh)

    def put_first(s, rows, value):
        strip[0, s + 1, rows, :] = value
        pairs[s, rows, :] = edges(value, value)

    wait_all(start_copies)
    take_rows(first, xr.at[0], HALO, HALO, 2 * SUB)
    build_strips(0, first, put_first)
    wrap_strips(strip.at[0])

    def forward(step):
        def body(s, carry):
            for r in blocks:
                rows, rows_e, rows_w = (slice(r + d, r + d + SUB) for d in (0, 1, -1))
                pair = pairs[s, rows, :]
                a, b, w = af[step, 0, rows, :], bf[step, 0, rows, :], wf[0, rows, :]
                for g in range(GROUPS):
                    c = g * each + s
                    value = state[step, c, rows, :]
                    side = side_of(pair, g)
                    c_s = jnp.where(first_lane, side, roll_lanes(value, 1))
                    c_n = jnp.where(last_lane, side, back(value, 1))
                    c_e, c_w = state[step, c, rows_e, :], state[step, c, rows_w, :]
                    vert = state[step, level_up(c), rows, :] + state[step, level_down(c), rows, :] - 2.0 * value
                    delta = c_n - c_s
                    if step < 2:
                        dy[step, c, rows, :] = delta
                    lap = c_e + c_w + c_n + c_s - 4.0 * value
                    d = diff_ref[c // levels, c % levels]
                    state[step + 1, c, rows, :] = value + w * (
                        d * lap - a * (c_e - c_w) - b * delta + VERTICAL_MIX * vert
                    )
                a, b, w = af[step, 1, rows, :], bf[step, 1, rows, :], wf[1, rows, :]
                value = strip[step, s + 1, rows, :]
                c_s, c_n = roll_lanes(value, 1), back(value, 1)
                c_e, c_w = strip[step, s + 1, rows_e, :], strip[step, s + 1, rows_w, :]
                delta = c_n - c_s
                if step < 2:
                    sdy[step, s, rows, :] = delta
                lap = c_e + c_w + c_n + c_s - 4.0 * value
                vert = strip_vertical(strip.at[step], s, rows, value)
                value = value + w * (sdiff[s] * lap - a * (c_e - c_w) - b * delta + VERTICAL_MIX * vert)
                strip[step + 1, s + 1, rows, :] = value
                pairs[s, rows, :] = edges(value, value)
            return carry

        over(body)

    outer_copies, fields_b = [], []
    for step in range(ITERS - 1):
        slopes(step, True)
        if step == 1:
            fields_b = send_fields(3, (hf[2, 0, own, :],))
        forward(step)
        if step == 1:
            outer_copies = send_rows(state.at[2], ys, yr, 2, 3 * HALO, 2 * HALO + 2)
            outer_copies += send_strips(2, state.at[2])
        if step < 2:
            wrap_strips(strip.at[step + 1])
    slopes(3, False)

    def last_sums(s, carry):
        total_u, total_v = carry
        pair = pairs[s, own, :]
        for g in range(GROUPS):
            c = g * each + s
            value = state[3, c, own, :]
            side = side_of(pair, g)
            m = wf[0, own, :] * lam[c, own, :]
            delta = jnp.where(last_lane, side, back(value, 1)) - jnp.where(first_lane, side, roll_lanes(value, 1))
            total_u = total_u + m * (state[3, c, SUB + 1:2 * SUB + 1, :] - state[3, c, SUB - 1:2 * SUB - 1, :])
            total_v = total_v + m * delta
        return total_u, total_v

    total_u, total_v = over(last_sums, (zero, zero))
    fields_c = send_fields(4, (total_u, total_v, hf[3, 0, own, :], af[3, 0, own, :]))

    def put_weight(s, rows, value):
        slam[s, rows, :] = value

    wait_all(weight_copies)
    take_rows(lam, xr.at[1], HALO, HALO, 2 * SUB)
    build_strips(1, lam, put_weight)

    def spread_pair(step, s, rows, m):
        bm = bf[step, 1, rows, :] * m
        dm = sdiff[s] * m
        pairs[s, rows, :] = edges(dm - bm, dm + bm)

    def put_outer(s, rows, value):
        sdy[2, s, rows, :] = back(value, 1) - roll_lanes(value, 1)
        strip[2, s + 1, rows, :] = value
        pairs[s, rows, :] = edges(value, value)

    wait_all(outer_copies)
    take_rows(state.at[2], yr, 2, HALO, 2 * SUB + 2)
    build_strips(2, state.at[2], put_outer)

    def outer_slopes(s, carry):
        for r in blocks:
            rows = slice(r, r + SUB)
            pair = pairs[s, rows, :]
            for g in range(GROUPS):
                c = g * each + s
                value = state[2, c, rows, :]
                side = side_of(pair, g)
                dy[2, c, rows, :] = (
                    jnp.where(last_lane, side, back(value, 1)) - jnp.where(first_lane, side, roll_lanes(value, 1))
                )
        return carry

    over(outer_slopes)
    wait_all(fields_b)
    take_field(3, hf.at[2])
    slopes(2, False)
    wait_all(fields_c)
    take_field(4, gu)
    take_field(5, gv)
    take_field(6, hf.at[3])
    slopes(3, False)
    take_field(7, af.at[3])
    for copy in a2a + sends:
        copy.wait_send()

    def weigh(s, carry):
        for r in blocks:
            rows = slice(r, r + SUB)
            for g in range(GROUPS):
                c = g * each + s
                mu[c, rows, :] = wf[0, rows, :] * lam[c, rows, :]
            m = wf[1, rows, :] * slam[s, rows, :]
            smu[s + 1, rows, :] = m
            spread_pair(3, s, rows, m)
        return carry

    def sums(step):
        def body(s, carry):
            result = []
            for r, (total_u, total_v, strip_u, strip_v) in zip(blocks, (carry[:4], carry[4:])):
                rows, rows_e, rows_w = (slice(r + d, r + d + SUB) for d in (0, 1, -1))
                w = wf[0, rows, :]
                for g in range(GROUPS):
                    c = g * each + s
                    m = w * lam[c, rows, :]
                    mu[c, rows, :] = m
                    total_u = total_u + m * (state[step, c, rows_e, :] - state[step, c, rows_w, :])
                    total_v = total_v + m * dy[step, c, rows, :]
                m = wf[1, rows, :] * slam[s, rows, :]
                smu[s + 1, rows, :] = m
                strip_u = strip_u + m * (strip[step, s + 1, rows_e, :] - strip[step, s + 1, rows_w, :])
                strip_v = strip_v + m * sdy[step, s, rows, :]
                spread_pair(step, s, rows, m)
                result += [total_u, total_v, strip_u, strip_v]
            return tuple(result)

        totals = over(body, (zero,) * 8)
        for r, (total_u, total_v, strip_u, strip_v) in zip(blocks, (totals[:4], totals[4:])):
            rows = slice(r, r + SUB)
            gu[0, rows, :], gv[0, rows, :] = total_u, total_v
            gu[1, rows, :], gv[1, rows, :] = everywhere(strip_u), everywhere(strip_v)

    def adjoint(step):
        last = step == 0

        def body(s, carry):
            for r in (SUB,) if last else blocks:
                rows, rows_e, rows_w = (slice(r + d, r + d + SUB) for d in (0, 1, -1))
                pair = pairs[s, rows, :]
                a_e, a_w, b = af[step, 0, rows_e, :], af[step, 0, rows_w, :], bf[step, 0, rows, :]
                push = prow[0, rows, :]
                for g in range(GROUPS):
                    c = g * each + s
                    m = mu[c, rows, :]
                    m_e, m_w = mu[c, rows_e, :], mu[c, rows_w, :]
                    vert = mu[level_up(c), rows, :] + mu[level_down(c), rows, :] - 2.0 * m
                    d = diff_ref[c // levels, c % levels]
                    bm = b * m
                    dm = d * m
                    side = side_of(pair, g)
                    from_s = jnp.where(first_lane, side, roll_lanes(dm - bm, 1))
                    from_n = jnp.where(last_lane, side, back(dm + bm, 1))
                    value = lam[c, rows, :] + VERTICAL_MIX * vert - 4.0 * dm + from_s + from_n
                    value = value + d * (m_w + m_e) + (a_e * m_e - a_w * m_w)
                    if c < levels:
                        value = value + push
                    if last:
                        out_ref[c] = value
                    else:
                        lam[c, rows, :] = value
                if last:
                    continue
                m, m_e, m_w = smu[s + 1, rows, :], smu[s + 1, rows_e, :], smu[s + 1, rows_w, :]
                bm = bf[step, 1, rows, :] * m
                dm = sdiff[s] * m
                value = slam[s, rows, :] + VERTICAL_MIX * strip_vertical(smu, s, rows, m) - 4.0 * dm
                value = value + roll_lanes(dm - bm, 1) + back(dm + bm, 1) + sdiff[s] * (m_w + m_e)
                value = value + (af[step, 1, rows_e, :] * m_e - af[step, 1, rows_w, :] * m_w)
                slam[s, rows, :] = value + jnp.where(channel_of(s) < levels, prow[1, rows, :], 0.0)
            return carry

        over(body)

    for step in reversed(range(ITERS)):
        if step == ITERS - 1:
            over(weigh)
        else:
            sums(step)
        wrap_strips(smu)
        results = []
        for g in blocks:
            rows = slice(g, g + SUB)
            parts = []
            for k in range(2):
                value = lh[k, rows, :]
                prow[k, rows, :] = (BUOYANCY / levels) * wf[k, rows, :] * value
                turn = (0.25 * ADVECTION) * gu[k, rows, :]
                spread = HEIGHT_DIFFUSION * value
                damp = jnp.tanh(hf[step, k, rows, :])
                kept = value - 4.0 * spread - HEIGHT_DAMPING * (1.0 - damp * damp) * value
                before, after = slice(g - 1, g - 1 + SUB), slice(g + 1, g + 1 + SUB)
                kept = kept + HEIGHT_DIFFUSION * (lh[k, before, :] + lh[k, after, :])
                kept = kept + (0.25 * ADVECTION) * (gv[k, after, :] - gv[k, before, :])
                parts.append((kept, spread + turn, spread - turn))
            (main, to_n, to_s), (piece, piece_n, piece_s) = parts
            side = side_of(edges(piece_n, piece_s), 0)
            main = main + jnp.where(first_lane, side, roll_lanes(to_n, 1)) + jnp.where(last_lane, side, back(to_s, 1))
            piece = piece + roll_lanes(piece_n, 1) + back(piece_s, 1)
            results.append((main, jnp.where(inside, piece, 0.0)))
        for g, result in zip(blocks, results):
            for k in range(2):
                lh[k, g:g + SUB, :] = result[k]
        adjoint(step)

    outh_ref[...] = lh[0, own, :]


def local(checkpoint, holder_list, height, land_mask, diffusivity, tracer_weight, height_weight):
    n, n_y = lax.axis_size("gx"), lax.axis_size("gy")
    width_x, width_y = height.shape
    assert (width_x, width_y) == (SUB, LANE)
    levels = diffusivity.shape[1]
    channels = 3 * levels
    each = channels // GROUPS
    piece_rows = checkpoint.shape[3] // LANE
    padded = -(-piece_rows // SUB) * SUB
    f32 = jnp.float32
    vmem = pl.BlockSpec(memory_space=pltpu.VMEM)
    tile = pltpu.VMEM((SUB, LANE), f32)
    field = pltpu.VMEM((2, 3 * SUB, LANE), f32)
    fields = pltpu.VMEM((ITERS, 2, 3 * SUB, LANE), f32)
    volume = pltpu.VMEM((channels, 3 * SUB, LANE), f32)

    def strips(*lead):
        return pltpu.VMEM((*lead, 3 * SUB, LANE), f32)

    half = channels * HALO // SUB
    out, out_h = pl.pallas_call(
        functools.partial(kernel, n, n_y, levels, piece_rows),
        out_shape=(pltpu.VMEM((channels, SUB, LANE), f32), pltpu.VMEM((SUB, LANE), f32)),
        in_specs=[pl.BlockSpec(memory_space=pltpu.HBM)] * 7,
        out_specs=(vmem, vmem),
        scratch_shapes=[
            pltpu.VMEM((n * padded, LANE), f32),
            pltpu.VMEM((n, padded, LANE), f32),
            pltpu.VMEM((ITERS, channels, 3 * SUB, LANE), f32),
            strips(ITERS, each + 2),
            volume, strips(each),
            volume, strips(each + 2),
            pltpu.VMEM((3, channels, 3 * SUB, LANE), f32), strips(3, each),
            strips(each),
            pltpu.VMEM((each, SUB, LANE), f32),
            fields, fields, fields,
            field, field, field, field, field,
            strips(8),
            pltpu.VMEM((8, SUB, LANE), f32),
            strips(2, 8),
            pltpu.VMEM((3, each // 2, SUB, LANE), f32),
            strips(3, 2, each // 2),
            pltpu.VMEM((2, 2, half, SUB, LANE), f32),
            pltpu.VMEM((2, 2, half, SUB, LANE), f32),
            pltpu.VMEM((2, half // 2, SUB, LANE), f32),
            pltpu.VMEM((2, half // 2, SUB, LANE), f32),
            pltpu.SMEM(holder_list.shape, jnp.int32),
            pltpu.SMEM(diffusivity.shape, f32),
            pltpu.VMEM(checkpoint.shape[2:], f32),
            tile,
            pltpu.VMEM((SUB, LANE), jnp.int32),
            tile,
            pltpu.SemaphoreType.DMA((n,)),
            pltpu.SemaphoreType.DMA((n,)),
            pltpu.SemaphoreType.DMA((48,)),
            pltpu.SemaphoreType.DMA((48,)),
            pltpu.SemaphoreType.DMA((7,)),
        ],
        compiler_params=pltpu.CompilerParams(
            collective_id=0, has_side_effects=True, vmem_limit_bytes=60 * 2**20
        ),
    )(
        holder_list, diffusivity, checkpoint.reshape(checkpoint.shape[2:]), height, land_mask,
        tracer_weight.reshape(channels, SUB, LANE), height_weight,
    )
    return out.reshape(tracer_weight.shape), out_h


def solution(mesh):
    return jax.shard_map(
        local,
        mesh=mesh,
        in_specs=(
            P(("member", "gx"), "gy", None, None),
            P(("member", "gx"), "gy", None),
            P(("member", "gx"), "gy"),
            P("gx", "gy"),
            P(),
            P("member", None, "gx", "gy"),
            P(("member", "gx"), "gy"),
        ),
        out_specs=(P("member", None, "gx", "gy"), P(("member", "gx"), "gy")),
        check_vma=False,
    )
```

```python
import functools
import jax
import jax.numpy as jnp
from jax import lax
from jax.experimental import pallas as pl
from jax.experimental.pallas import tpu as pltpu
from jax.sharding import PartitionSpec as P

ITERS = 4
ADVECTION = 0.3
VERTICAL_MIX = 0.1
HEIGHT_DIFFUSION = 0.2
HEIGHT_DAMPING = 0.3
BUOYANCY = 0.5

SUB = 8
LANE = 128
HALO = 4
GROUP = 16
GROUPS = LANE // GROUP
MESH = pl.DeviceIdType.MESH


def roll_lanes(value, shift):
    return pltpu.roll(value, shift, 1)


def roll_rows(value, shift):
    return pltpu.roll(value, shift, 0)


def kernel(
    n, n_y, levels, piece_rows,
    holder_hbm, diff_hbm, ckpt_hbm, height_hbm, mask_hbm, tw_hbm, hw_hbm,
    out_ref, outh_ref,
    buf, recv, state, strip, lam, slam, mu, smu, dy, sdy, pairs, sdiff,
    hf, af, bf, wf, lh, gu, gv, prow,
    em, es, el, zq, zl, xs, xr, ys, yr,
    holder_ref, diff_ref, ckpt_ref, height_ref, mask_ref, hw_ref,
    a2a_send, a2a_recv, send_sem, recv_sem, in_sem,
):
    me = lax.axis_index("gx")
    my = lax.axis_index("gy")
    east, west = lax.rem(me + 1, n), lax.rem(me + n - 1, n)
    north, south = lax.rem(my + 1, n_y), lax.rem(my + n_y - 1, n_y)
    channels = 3 * levels
    each = channels // GROUPS
    padded = -(-piece_rows // SUB) * SUB
    own = slice(SUB, 2 * SUB)
    blocks = (HALO, HALO + SUB)

    inputs = (
        (ckpt_hbm, ckpt_ref), (diff_hbm, diff_ref), (mask_hbm, mask_ref), (tw_hbm, lam.at[:, pl.ds(SUB, SUB)]),
        (height_hbm, height_ref), (hw_hbm, hw_ref), (holder_hbm, holder_ref),
    )
    loads = [pltpu.make_async_copy(source, target, in_sem.at[i]) for i, (source, target) in enumerate(inputs)]
    for load in loads:
        load.start()

    barrier = pltpu.get_barrier_semaphore()
    for k in range(1, n):
        pl.semaphore_signal(barrier, inc=1, device_id={"gx": lax.rem(me + k, n)}, device_id_type=MESH)
    for other in (north, south):
        pl.semaphore_signal(barrier, inc=1, device_id={"gy": other}, device_id_type=MESH)
        for side in (east, west):
            pl.semaphore_signal(barrier, inc=1, device_id={"gx": side, "gy": other}, device_id_type=MESH)

    loads[0].wait()
    if padded != piece_rows:
        buf[...] = jnp.zeros_like(buf)
    for o in range(0, n, SUB):
        size = min(SUB, n - o)
        for r in range(piece_rows):
            buf[pl.ds(o * padded + r, size, stride=padded), :] = ckpt_ref[o:o + size, r * LANE:(r + 1) * LANE]

    pl.semaphore_wait(barrier, n + 5)

    mine = pl.multiple_of(me * padded, SUB)
    sends = []
    a2a = []
    for k in range(1, n):
        owner = lax.rem(me + k, n)
        copy = pltpu.make_async_remote_copy(
            src_ref=buf.at[pl.ds(pl.multiple_of(owner * padded, SUB), padded)],
            dst_ref=recv.at[me],
            send_sem=a2a_send.at[k], recv_sem=a2a_recv.at[k],
            device_id={"gx": owner}, device_id_type=MESH,
        )
        copy.start()
        a2a.append(copy)
    recv[me] = buf[pl.ds(mine, padded), :]

    used = [0]

    def send(source, target, device):
        i = used[0]
        used[0] += 1
        copy = pltpu.make_async_remote_copy(
            src_ref=source, dst_ref=target, send_sem=send_sem.at[i], recv_sem=recv_sem.at[i],
            device_id=device, device_id_type=MESH,
        )
        copy.start()
        sends.append(copy)
        return copy

    def wait_all(copies):
        for copy in copies:
            copy.wait_recv()

    lane = lax.broadcasted_iota(jnp.int32, (SUB, LANE), 1)
    sub = lax.broadcasted_iota(jnp.int32, (SUB, LANE), 0)
    first_lane, last_lane = lane == 0, lane == LANE - 1
    group = lax.shift_right_logical(lane, 4)
    place = lane & (GROUP - 1)
    low, high = place < HALO, place >= GROUP - HALO
    half = place < GROUP // 2
    edge = place == HALO - 1
    below, above = jnp.where(low, my, 1), jnp.where(high, n_y - 1 - my, 1)
    inside = (below > 0) & (above > 0)
    zero = jnp.zeros((SUB, LANE), jnp.float32)

    def back(value, shift):
        return roll_lanes(value, (LANE - shift) % LANE)

    def everywhere(value):
        moved = [value] + [roll_lanes(value, GROUP * k) for k in range(1, GROUPS)]
        while len(moved) > 1:
            moved = [a + b for a, b in zip(moved[::2], moved[1::2])]
        return moved[0]

    def edges(from_south, from_north):
        return jnp.where(edge, from_south, back(from_north, GROUP - 2 * HALO + 2))

    def side_of(pair, g):
        return back(pair, g * GROUP + HALO - 1)

    def channel_of(s):
        return group * each + s

    def first_level(s):
        return (channel_of(s) & (levels - 1)) == 0

    def last_level(s):
        return (channel_of(s) & (levels - 1)) == levels - 1

    def level_up(c):
        return c - 1 if c % levels else c

    def level_down(c):
        return c + 1 if (c + 1) % levels else c

    def over(body, carry=0):
        for s in range(each):
            carry = body(s, carry)
        return carry

    def pack_field(value):
        south_part = (lane >= HALO) & (lane < 2 * HALO)
        north_part = (lane >= 2 * HALO) & (lane < 3 * HALO)
        picked = jnp.where(south_part, roll_lanes(value, HALO), jnp.where(north_part, roll_lanes(value, 3 * HALO), 0.0))
        return everywhere(picked)

    outer = (slice(0, SUB), slice(2 * SUB, 3 * SUB))

    def both(ref):
        return jnp.where(sub < HALO, ref[outer[1], :], ref[outer[0], :])

    def fetch(ref, rows):
        return both(ref) if rows is outer else ref[rows, :]

    def place_at(ref, rows, value):
        for part in rows if rows is outer else (rows,):
            ref[part, :] = value

    def pack_strip(ref, s, rows):
        packed = zero
        for g in range(GROUPS):
            moved = roll_lanes(fetch(ref.at[g * each + s], rows), (g * GROUP + 2 * HALO) % LANE)
            packed = jnp.where(group == g, moved, packed)
        return packed

    lower_half, upper_half = pl.ds(0, HALO), pl.ds(HALO, HALO)
    before, after = pl.ds(HALO, HALO), pl.ds(4 * HALO, HALO)

    def send_strips(which, ref, hold=None):
        def body(q, carry):
            a, b = pack_strip(ref, 2 * q, own), pack_strip(ref, 2 * q + 1, own)
            if hold is not None:
                hold[2 * q + 1, own, :], hold[2 * q + 2, own, :] = a, b
            zq[which, q] = jnp.where(half, back(a, HALO), roll_lanes(b, HALO))
            return carry

        lax.fori_loop(0, each // 2, body, 0, unroll=True)
        copies = []
        for side, other in enumerate((north, south)):
            for source, target, device in (
                (pl.ds(0, SUB), pl.ds(SUB, SUB), {"gy": other}),
                (upper_half, before, {"gx": east, "gy": other}),
                (lower_half, after, {"gx": west, "gy": other}),
            ):
                copies.append(send(zq.at[which, :, source], zl.at[which, side, :, target], device))
        return copies

    def merge(which, s, rows, packed):
        q, odd = s // 2, s % 2
        from_south, from_north = fetch(zl.at[which, 0, q], rows), fetch(zl.at[which, 1, q], rows)
        if odd:
            from_south = back(from_south, GROUP // 2)
        else:
            from_north = roll_lanes(from_north, GROUP // 2)
        mid = jnp.where(half, back(packed, HALO), roll_lanes(packed, HALO))
        value = jnp.where(low, from_south, jnp.where(high, from_north, mid))
        return jnp.where(inside, value, 0.0)

    def build_strips(which, ref, put):
        for s in range(each):
            for g in blocks:
                rows = slice(g, g + SUB)
                put(s, rows, merge(which, s, rows, pack_strip(ref, s, rows)))

    def send_rows(ref, out, into, width, to_east, to_west):
        count = channels * width // SUB
        place_of = lax.div(sub, width)
        for side, start in enumerate((to_east, to_west)):
            def body(k, carry):
                value = zero
                for j in range(SUB // width):
                    rows = slice(start - width * j, start - width * j + SUB)
                    value = jnp.where(place_of == j, ref[k + j * count, rows, :], value)
                out[side, k] = value
                return carry

            lax.fori_loop(0, count, body, 0, unroll=4)
        return [send(out.at[0], into.at[0], {"gx": east}), send(out.at[1], into.at[1], {"gx": west})]

    def take_rows(ref, into, width, from_west, from_east):
        count = channels * width // SUB

        def body(k, carry):
            for side, (base, offset) in enumerate(((0, from_west), (2 * SUB, from_east - 2 * SUB))):
                value = into[side, k]
                rows = slice(base, base + SUB)
                mask = (sub >= offset) & (sub < offset + width)
                for j in range(SUB // width):
                    shift = (offset - width * j) % SUB
                    c = k + j * count
                    ref[c, rows, :] = jnp.where(mask, roll_rows(value, shift) if shift else value, ref[c, rows, :])
            return carry

        lax.fori_loop(0, count, body, 0, unroll=4)

    def send_direct(ref):
        return [
            send(ref.at[:, pl.ds(3 * HALO, HALO)], ref.at[:, pl.ds(HALO, HALO)], {"gx": east}),
            send(ref.at[:, pl.ds(2 * HALO, HALO)], ref.at[:, pl.ds(4 * HALO, HALO)], {"gx": west}),
        ]

    def send_fields(first, values):
        for k, value in enumerate(values):
            em[first + k, own, :] = value
            es[first + k] = pack_field(value)
        which = pl.ds(first, len(values))
        copies = [
            send(em.at[which, pl.ds(3 * HALO, HALO)], em.at[which, before], {"gx": east}),
            send(em.at[which, pl.ds(2 * HALO, HALO)], em.at[which, after], {"gx": west}),
        ]
        for side, other in enumerate((north, south)):
            copies.append(send(es.at[which], el.at[side, which, pl.ds(SUB, SUB)], {"gy": other}))
            copies.append(send(es.at[which, upper_half], el.at[side, which, before], {"gx": east, "gy": other}))
            copies.append(send(es.at[which, lower_half], el.at[side, which, after], {"gx": west, "gy": other}))
        return copies

    def take_field(k, target):
        for r in range(0, 3 * SUB, SUB):
            rows = slice(r, r + SUB)
            value = em[k, rows, :]
            piece = jnp.where(
                low, back(el[0, k, rows, :], GROUP // 2),
                jnp.where(high, roll_lanes(el[1, k, rows, :], GROUP // 2), pack_field(value)),
            )
            target[0, rows, :] = value
            target[1, rows, :] = jnp.where(inside, piece, 0.0)

    def along(field, g, shift):
        return field[0, g + shift:g + shift + SUB, :], field[1, g + shift:g + shift + SUB, :]

    def latitude(main, piece):
        side = side_of(edges(piece, piece), 0)
        h_n = jnp.where(last_lane, side, back(main, 1))
        h_s = jnp.where(first_lane, side, roll_lanes(main, 1))
        return h_n, h_s, back(piece, 1), roll_lanes(piece, 1)

    def total_of(step, rows):
        main = state[step, 0, rows, :]
        for c in range(1, levels):
            main = main + state[step, c, rows, :]
        piece = zero
        for s in range(each):
            piece = piece + jnp.where(channel_of(s) < levels, strip[step, s + 1, rows, :], 0.0)
        return main, everywhere(piece)

    def slopes(step, advance):
        for g in blocks:
            rows = slice(g, g + SUB)
            main, piece = along(hf.at[step], g, 0)
            main_e, piece_e = along(hf.at[step], g, 1)
            main_w, piece_w = along(hf.at[step], g, -1)
            main_n, main_s, piece_n, piece_s = latitude(main, piece)
            af[step, 0, rows, :] = (-0.25 * ADVECTION) * (main_n - main_s)
            af[step, 1, rows, :] = (-0.25 * ADVECTION) * (piece_n - piece_s)
            bf[step, 0, rows, :] = (0.25 * ADVECTION) * (main_e - main_w)
            bf[step, 1, rows, :] = (0.25 * ADVECTION) * (piece_e - piece_w)
            if not advance:
                continue
            totals = total_of(step, rows)
            for k, (h, h_e, h_w, h_n, h_s) in enumerate((
                (main, main_e, main_w, main_n, main_s), (piece, piece_e, piece_w, piece_n, piece_s),
            )):
                lap = h_e + h_w + h_n + h_s - 4.0 * h
                value = h + HEIGHT_DIFFUSION * lap - HEIGHT_DAMPING * jnp.tanh(h)
                value = value + (BUOYANCY / levels) * wf[k, rows, :] * totals[k]
                hf[step + 1, k, rows, :] = jnp.where(inside, value, 0.0) if k else value

    def wrap_strips(ref):
        for g in blocks:
            rows = slice(g, g + SUB)
            ref[0, rows, :] = roll_lanes(ref[each, rows, :], GROUP)
            ref[each + 1, rows, :] = back(ref[1, rows, :], GROUP)

    def strip_vertical(ref, s, rows, value):
        upper = jnp.where(first_level(s), value, ref[s, rows, :])
        lower = jnp.where(last_level(s), value, ref[s + 2, rows, :])
        return upper + lower - 2.0 * value

    for load in loads[1:]:
        load.wait()
    fields_a = send_fields(0, (height_ref[...], mask_ref[...].astype(jnp.float32), hw_ref[...]))

    for s in range(each):
        value = zero
        for g in range(GROUPS):
            c = g * each + s
            value = jnp.where(group == g, diff_ref[c // levels, c % levels], value)
        sdiff[s] = value
    for step in range(1, ITERS):
        for k in range(2):
            hf[step, k, 0:SUB, :] = zero
            hf[step, k, 2 * SUB:3 * SUB, :] = zero
    for k in range(2):
        for r in range(0, 3 * SUB, SUB):
            gu[k, r:r + SUB, :] = zero
            gv[k, r:r + SUB, :] = zero

    for copy in a2a:
        copy.wait_recv()
    first = state.at[0]
    for p in range(n):
        holder = holder_ref[0, 0, p]
        if piece_rows % SUB == 0:
            depth = piece_rows // SUB
            for c in range(depth):
                first[p * depth + c, own, :] = recv[holder, c * SUB:(c + 1) * SUB, :]
        else:
            for r in range(piece_rows):
                row = p * piece_rows + r
                at = SUB + row % SUB
                first[row // SUB, at:at + 1, :] = recv[holder, r:r + 1, :]

    start_copies = send_direct(first)
    edge_copies = send_strips(0, first, strip.at[0])
    weight_copies = send_direct(lam)
    weight_copies += send_strips(1, lam)

    wait_all(fields_a)
    take_field(0, hf.at[0])
    take_field(1, wf)
    take_field(2, lh)

    def put_first(s, rows, value):
        place_at(strip.at[0, s + 1], rows, value)
        place_at(pairs.at[s], rows, edges(value, value))

    def roll_pass(step, s, rows):
        pair = fetch(pairs.at[s], rows)
        for g in range(GROUPS):
            c = g * each + s
            value = fetch(state.at[step, c], rows)
            side = side_of(pair, g)
            c_s = jnp.where(first_lane, side, roll_lanes(value, 1))
            c_n = jnp.where(last_lane, side, back(value, 1))
            place_at(dy.at[step, c], rows, c_n - c_s)
            place_at(mu.at[c], rows, c_n + c_s)
        value = fetch(strip.at[step, s + 1], rows)
        c_s, c_n = roll_lanes(value, 1), back(value, 1)
        place_at(sdy.at[step, s], rows, c_n - c_s)
        place_at(smu.at[s], rows, c_n + c_s)

    def inner_rolls(s, carry):
        roll_pass(0, s, own)
        return carry

    def outer_rolls(s, carry):
        roll_pass(0, s, outer)
        return carry

    wait_all(edge_copies[0::3])
    for s in range(each):
        put_first(s, own, merge(0, s, own, strip[0, s + 1, own, :]))
    lax.fori_loop(0, each, inner_rolls, 0, unroll=3)
    wait_all(edge_copies[1::3] + edge_copies[2::3])
    wait_all(start_copies)
    for s in range(each):
        put_first(s, outer, merge(0, s, outer, pack_strip(first, s, outer)))
    lax.fori_loop(0, each, outer_rolls, 0, unroll=3)
    wrap_strips(strip.at[0])

    def forward(step):
        def roll_body(s, carry):
            for r in blocks:
                roll_pass(step, s, slice(r, r + SUB))
            return carry

        if step:
            lax.fori_loop(0, each, roll_body, 0, unroll=3)
        for s in range(each):
            for r in blocks:
                rows, rows_e, rows_w = (slice(r + d, r + d + SUB) for d in (0, 1, -1))
                a, b, w = af[step, 0, rows, :], bf[step, 0, rows, :], wf[0, rows, :]
                for g in range(GROUPS):
                    c = g * each + s
                    value = state[step, c, rows, :]
                    c_e, c_w = state[step, c, rows_e, :], state[step, c, rows_w, :]
                    levels_sum = state[step, level_up(c), rows, :] + state[step, level_down(c), rows, :]
                    d = diff_ref[c // levels, c % levels]
                    change = d * (c_e + c_w + mu[c, rows, :]) + VERTICAL_MIX * levels_sum
                    change = change - (4.0 * d + 2.0 * VERTICAL_MIX) * value
                    state[step + 1, c, rows, :] = value + w * (change - a * (c_e - c_w) - b * dy[step, c, rows, :])
                a, b, w = af[step, 1, rows, :], bf[step, 1, rows, :], wf[1, rows, :]
                value = strip[step, s + 1, rows, :]
                c_e, c_w = strip[step, s + 1, rows_e, :], strip[step, s + 1, rows_w, :]
                lap = c_e + c_w + smu[s, rows, :] - 4.0 * value
                vert = strip_vertical(strip.at[step], s, rows, value)
                value = value + w * (sdiff[s] * lap - a * (c_e - c_w) - b * sdy[step, s, rows, :] + VERTICAL_MIX * vert)
                strip[step + 1, s + 1, rows, :] = value
                pairs[s, rows, :] = edges(value, value)

    outer_copies, fields_b = [], []
    for step in range(ITERS - 1):
        slopes(step, True)
        if step == 1:
            pass
        forward(step)
        if step == 1:
            outer_copies = send_rows(state.at[2], ys, yr, 2, 3 * HALO, 2 * HALO + 2)
            outer_copies += send_strips(2, state.at[2])
        if step < 2:
            wrap_strips(strip.at[step + 1])
    slopes(3, False)

    def last_sums(s, carry):
        total_u, total_v = carry
        pair = pairs[s, own, :]
        for g in range(GROUPS):
            c = g * each + s
            value = state[3, c, own, :]
            side = side_of(pair, g)
            m = wf[0, own, :] * lam[c, own, :]
            delta = jnp.where(last_lane, side, back(value, 1)) - jnp.where(first_lane, side, roll_lanes(value, 1))
            total_u = total_u + m * (state[3, c, SUB + 1:2 * SUB + 1, :] - state[3, c, SUB - 1:2 * SUB - 1, :])
            total_v = total_v + m * delta
        return total_u, total_v

    total_u, total_v = over(last_sums, (zero, zero))
    fields_c = send_fields(3, (hf[2, 0, own, :], total_u, total_v, hf[3, 0, own, :]))

    def put_weight(s, rows, value):
        slam[s, rows, :] = value

    wait_all(weight_copies)
    build_strips(1, lam, put_weight)

    def spread_pair(step, s, rows, m):
        bm = bf[step, 1, rows, :] * m
        dm = sdiff[s] * m
        pairs[s, rows, :] = edges(dm - bm, dm + bm)

    def put_outer(s, rows, value):
        sdy[2, s, rows, :] = back(value, 1) - roll_lanes(value, 1)
        strip[2, s + 1, rows, :] = value
        pairs[s, rows, :] = edges(value, value)

    wait_all(outer_copies)
    take_rows(state.at[2], yr, 2, HALO, 2 * SUB + 2)
    build_strips(2, state.at[2], put_outer)

    def outer_slopes(s, carry):
        for r in blocks:
            rows = slice(r, r + SUB)
            pair = pairs[s, rows, :]
            for g in range(GROUPS):
                c = g * each + s
                value = state[2, c, rows, :]
                side = side_of(pair, g)
                dy[2, c, rows, :] = (
                    jnp.where(last_lane, side, back(value, 1)) - jnp.where(first_lane, side, roll_lanes(value, 1))
                )
        return carry

    over(outer_slopes)
    def weigh(s, carry):
        for r in blocks:
            rows = slice(r, r + SUB)
            for g in range(GROUPS):
                c = g * each + s
                mu[c, rows, :] = wf[0, rows, :] * lam[c, rows, :]
            smu[s + 1, rows, :] = wf[1, rows, :] * slam[s, rows, :]
        return carry

    over(weigh)
    wrap_strips(smu)
    wait_all(fields_c)
    take_field(3, hf.at[2])
    slopes(2, False)
    take_field(4, gu)
    take_field(5, gv)
    take_field(6, hf.at[3])
    slopes(3, False)
    for copy in a2a + sends:
        copy.wait_send()

    def sums(step):
        def body(s, carry):
            result = []
            for r, (total_u, total_v, strip_u, strip_v) in zip(blocks, (carry[:4], carry[4:])):
                rows, rows_e, rows_w = (slice(r + d, r + d + SUB) for d in (0, 1, -1))
                w = wf[0, rows, :]
                for g in range(GROUPS):
                    c = g * each + s
                    m = w * lam[c, rows, :]
                    mu[c, rows, :] = m
                    total_u = total_u + m * (state[step, c, rows_e, :] - state[step, c, rows_w, :])
                    total_v = total_v + m * dy[step, c, rows, :]
                m = wf[1, rows, :] * slam[s, rows, :]
                smu[s + 1, rows, :] = m
                strip_u = strip_u + m * (strip[step, s + 1, rows_e, :] - strip[step, s + 1, rows_w, :])
                strip_v = strip_v + m * sdy[step, s, rows, :]
                spread_pair(step, s, rows, m)
                result += [total_u, total_v, strip_u, strip_v]
            return tuple(result)

        totals = over(body, (zero,) * 8)
        for r, (total_u, total_v, strip_u, strip_v) in zip(blocks, (totals[:4], totals[4:])):
            rows = slice(r, r + SUB)
            gu[0, rows, :], gv[0, rows, :] = total_u, total_v
            gu[1, rows, :], gv[1, rows, :] = everywhere(strip_u), everywhere(strip_v)

    def adjoint(step):
        last = step == 0

        def body(s, carry):
            for r in (SUB,) if last else blocks:
                rows, rows_e, rows_w = (slice(r + d, r + d + SUB) for d in (0, 1, -1))
                pair = pairs[s, rows, :]
                a_e, a_w, b = af[step, 0, rows_e, :], af[step, 0, rows_w, :], bf[step, 0, rows, :]
                push = prow[0, rows, :]
                for g in range(GROUPS):
                    c = g * each + s
                    m = mu[c, rows, :]
                    m_e, m_w = mu[c, rows_e, :], mu[c, rows_w, :]
                    vert = mu[level_up(c), rows, :] + mu[level_down(c), rows, :] - 2.0 * m
                    d = diff_ref[c // levels, c % levels]
                    bm = b * m
                    dm = d * m
                    side = side_of(pair, g)
                    from_s = jnp.where(first_lane, side, roll_lanes(dm - bm, 1))
                    from_n = jnp.where(last_lane, side, back(dm + bm, 1))
                    value = lam[c, rows, :] + VERTICAL_MIX * vert - 4.0 * dm + from_s + from_n
                    value = value + d * (m_w + m_e) + (a_e * m_e - a_w * m_w)
                    if c < levels:
                        value = value + push
                    if last:
                        out_ref[c] = value
                    else:
                        lam[c, rows, :] = value
                if last:
                    continue
                m, m_e, m_w = smu[s + 1, rows, :], smu[s + 1, rows_e, :], smu[s + 1, rows_w, :]
                bm = bf[step, 1, rows, :] * m
                dm = sdiff[s] * m
                value = slam[s, rows, :] + VERTICAL_MIX * strip_vertical(smu, s, rows, m) - 4.0 * dm
                value = value + roll_lanes(dm - bm, 1) + back(dm + bm, 1) + sdiff[s] * (m_w + m_e)
                value = value + (af[step, 1, rows_e, :] * m_e - af[step, 1, rows_w, :] * m_w)
                slam[s, rows, :] = value + jnp.where(channel_of(s) < levels, prow[1, rows, :], 0.0)
            return carry

        over(body)

    for step in reversed(range(ITERS)):
        if step == ITERS - 1:
            for s in range(each):
                for r in blocks:
                    rows = slice(r, r + SUB)
                    spread_pair(3, s, rows, smu[s + 1, rows, :])
        else:
            sums(step)
            wrap_strips(smu)
        results = []
        for g in blocks:
            rows = slice(g, g + SUB)
            parts = []
            for k in range(2):
                value = lh[k, rows, :]
                prow[k, rows, :] = (BUOYANCY / levels) * wf[k, rows, :] * value
                turn = (0.25 * ADVECTION) * gu[k, rows, :]
                spread = HEIGHT_DIFFUSION * value
                damp = jnp.tanh(hf[step, k, rows, :])
                kept = value - 4.0 * spread - HEIGHT_DAMPING * (1.0 - damp * damp) * value
                before, after = slice(g - 1, g - 1 + SUB), slice(g + 1, g + 1 + SUB)
                kept = kept + HEIGHT_DIFFUSION * (lh[k, before, :] + lh[k, after, :])
                kept = kept + (0.25 * ADVECTION) * (gv[k, after, :] - gv[k, before, :])
                parts.append((kept, spread + turn, spread - turn))
            (main, to_n, to_s), (piece, piece_n, piece_s) = parts
            side = side_of(edges(piece_n, piece_s), 0)
            main = main + jnp.where(first_lane, side, roll_lanes(to_n, 1)) + jnp.where(last_lane, side, back(to_s, 1))
            piece = piece + roll_lanes(piece_n, 1) + back(piece_s, 1)
            results.append((main, jnp.where(inside, piece, 0.0)))
        for g, result in zip(blocks, results):
            for k in range(2):
                lh[k, g:g + SUB, :] = result[k]
        adjoint(step)

    outh_ref[...] = lh[0, own, :]


def local(checkpoint, holder_list, height, land_mask, diffusivity, tracer_weight, height_weight):
    n, n_y = lax.axis_size("gx"), lax.axis_size("gy")
    width_x, width_y = height.shape
    assert (width_x, width_y) == (SUB, LANE)
    levels = diffusivity.shape[1]
    channels = 3 * levels
    each = channels // GROUPS
    piece_rows = checkpoint.shape[3] // LANE
    padded = -(-piece_rows // SUB) * SUB
    f32 = jnp.float32
    vmem = pl.BlockSpec(memory_space=pltpu.VMEM)
    tile = pltpu.VMEM((SUB, LANE), f32)
    field = pltpu.VMEM((2, 3 * SUB, LANE), f32)
    fields = pltpu.VMEM((ITERS, 2, 3 * SUB, LANE), f32)
    volume = pltpu.VMEM((channels, 3 * SUB, LANE), f32)

    def strips(*lead):
        return pltpu.VMEM((*lead, 3 * SUB, LANE), f32)

    half = channels * HALO // SUB
    out, out_h = pl.pallas_call(
        functools.partial(kernel, n, n_y, levels, piece_rows),
        out_shape=(pltpu.VMEM((channels, SUB, LANE), f32), pltpu.VMEM((SUB, LANE), f32)),
        in_specs=[pl.BlockSpec(memory_space=pltpu.HBM)] * 7,
        out_specs=(vmem, vmem),
        scratch_shapes=[
            pltpu.VMEM((n * padded, LANE), f32),
            pltpu.VMEM((n, padded, LANE), f32),
            pltpu.VMEM((ITERS, channels, 3 * SUB, LANE), f32),
            strips(ITERS, each + 2),
            volume, strips(each),
            volume, strips(each + 2),
            pltpu.VMEM((3, channels, 3 * SUB, LANE), f32), strips(3, each),
            strips(each),
            pltpu.VMEM((each, SUB, LANE), f32),
            fields, fields, fields,
            field, field, field, field, field,
            strips(8),
            pltpu.VMEM((8, SUB, LANE), f32),
            strips(2, 8),
            pltpu.VMEM((3, each // 2, SUB, LANE), f32),
            strips(3, 2, each // 2),
            pltpu.VMEM((2, 2, half, SUB, LANE), f32),
            pltpu.VMEM((2, 2, half, SUB, LANE), f32),
            pltpu.VMEM((2, half // 2, SUB, LANE), f32),
            pltpu.VMEM((2, half // 2, SUB, LANE), f32),
            pltpu.SMEM(holder_list.shape, jnp.int32),
            pltpu.SMEM(diffusivity.shape, f32),
            pltpu.VMEM(checkpoint.shape[2:], f32),
            tile,
            pltpu.VMEM((SUB, LANE), jnp.int32),
            tile,
            pltpu.SemaphoreType.DMA((n,)),
            pltpu.SemaphoreType.DMA((n,)),
            pltpu.SemaphoreType.DMA((48,)),
            pltpu.SemaphoreType.DMA((48,)),
            pltpu.SemaphoreType.DMA((7,)),
        ],
        compiler_params=pltpu.CompilerParams(
            collective_id=0, has_side_effects=True, vmem_limit_bytes=60 * 2**20
        ),
    )(
        holder_list, diffusivity, checkpoint.reshape(checkpoint.shape[2:]), height, land_mask,
        tracer_weight.reshape(channels, SUB, LANE), height_weight,
    )
    return out.reshape(tracer_weight.shape), out_h


def solution(mesh):
    return jax.shard_map(
        local,
        mesh=mesh,
        in_specs=(
            P(("member", "gx"), "gy", None, None),
            P(("member", "gx"), "gy", None),
            P(("member", "gx"), "gy"),
            P("gx", "gy"),
            P(),
            P("member", None, "gx", "gy"),
            P(("member", "gx"), "gy"),
        ),
        out_specs=(P("member", None, "gx", "gy"), P(("member", "gx"), "gy")),
        check_vma=False,
    )
```

```python
import functools
import jax
import jax.numpy as jnp
from jax import lax
from jax.experimental import pallas as pl
from jax.experimental.pallas import tpu as pltpu
from jax.sharding import PartitionSpec as P

ITERS = 4
ADVECTION = 0.3
VERTICAL_MIX = 0.1
HEIGHT_DIFFUSION = 0.2
HEIGHT_DAMPING = 0.3
BUOYANCY = 0.5

SUB = 8
LANE = 128
HALO = 4
GROUP = 16
GROUPS = LANE // GROUP
MESH = pl.DeviceIdType.MESH


def roll_lanes(value, shift):
    return pltpu.roll(value, shift, 1)


def roll_rows(value, shift):
    return pltpu.roll(value, shift, 0)


def kernel(
    n, n_y, levels, piece_rows,
    holder_hbm, diff_hbm, ckpt_hbm, height_hbm, mask_hbm, tw_hbm, hw_hbm,
    out_ref, outh_ref,
    buf, recv, state, strip, lam, slam, mu, smu, dy, sdy, pairs, sdiff,
    hf, af, bf, wf, lh, gu, gv, prow,
    em, es, el, zq, zl, xs, xr, ys, yr,
    holder_ref, diff_ref, ckpt_ref, height_ref, mask_ref, hw_ref,
    a2a_send, a2a_recv, send_sem, recv_sem, in_sem,
):
    me = lax.axis_index("gx")
    my = lax.axis_index("gy")
    east, west = lax.rem(me + 1, n), lax.rem(me + n - 1, n)
    north, south = lax.rem(my + 1, n_y), lax.rem(my + n_y - 1, n_y)
    channels = 3 * levels
    each = channels // GROUPS
    padded = -(-piece_rows // SUB) * SUB
    own = slice(SUB, 2 * SUB)
    blocks = (HALO, HALO + SUB)

    inputs = (
        (ckpt_hbm, ckpt_ref), (diff_hbm, diff_ref), (mask_hbm, mask_ref), (tw_hbm, lam.at[:, pl.ds(SUB, SUB)]),
        (height_hbm, height_ref), (hw_hbm, hw_ref), (holder_hbm, holder_ref),
    )
    loads = [pltpu.make_async_copy(source, target, in_sem.at[i]) for i, (source, target) in enumerate(inputs)]
    for load in loads:
        load.start()

    barrier = pltpu.get_barrier_semaphore()
    for k in range(1, n):
        pl.semaphore_signal(barrier, inc=1, device_id={"gx": lax.rem(me + k, n)}, device_id_type=MESH)
    for other in (north, south):
        pl.semaphore_signal(barrier, inc=1, device_id={"gy": other}, device_id_type=MESH)
        for side in (east, west):
            pl.semaphore_signal(barrier, inc=1, device_id={"gx": side, "gy": other}, device_id_type=MESH)

    loads[0].wait()
    if padded != piece_rows:
        buf[...] = jnp.zeros_like(buf)
    for o in range(0, n, SUB):
        size = min(SUB, n - o)
        for r in range(piece_rows):
            buf[pl.ds(o * padded + r, size, stride=padded), :] = ckpt_ref[o:o + size, r * LANE:(r + 1) * LANE]

    pl.semaphore_wait(barrier, n + 5)

    mine = pl.multiple_of(me * padded, SUB)
    sends = []
    a2a = []
    for k in range(1, n):
        owner = lax.rem(me + k, n)
        copy = pltpu.make_async_remote_copy(
            src_ref=buf.at[pl.ds(pl.multiple_of(owner * padded, SUB), padded)],
            dst_ref=recv.at[me],
            send_sem=a2a_send.at[k], recv_sem=a2a_recv.at[k],
            device_id={"gx": owner}, device_id_type=MESH,
        )
        copy.start()
        a2a.append(copy)
    recv[me] = buf[pl.ds(mine, padded), :]

    used = [0]

    def send(source, target, device):
        i = used[0]
        used[0] += 1
        copy = pltpu.make_async_remote_copy(
            src_ref=source, dst_ref=target, send_sem=send_sem.at[i], recv_sem=recv_sem.at[i],
            device_id=device, device_id_type=MESH,
        )
        copy.start()
        sends.append(copy)
        return copy

    def wait_all(copies):
        for copy in copies:
            copy.wait_recv()

    lane = lax.broadcasted_iota(jnp.int32, (SUB, LANE), 1)
    sub = lax.broadcasted_iota(jnp.int32, (SUB, LANE), 0)
    first_lane, last_lane = lane == 0, lane == LANE - 1
    group = lax.shift_right_logical(lane, 4)
    place = lane & (GROUP - 1)
    low, high = place < HALO, place >= GROUP - HALO
    half = place < GROUP // 2
    edge = place == HALO - 1
    below, above = jnp.where(low, my, 1), jnp.where(high, n_y - 1 - my, 1)
    inside = (below > 0) & (above > 0)
    zero = jnp.zeros((SUB, LANE), jnp.float32)

    def back(value, shift):
        return roll_lanes(value, (LANE - shift) % LANE)

    def everywhere(value):
        moved = [value] + [roll_lanes(value, GROUP * k) for k in range(1, GROUPS)]
        while len(moved) > 1:
            moved = [a + b for a, b in zip(moved[::2], moved[1::2])]
        return moved[0]

    def edges(from_south, from_north):
        return jnp.where(edge, from_south, back(from_north, GROUP - 2 * HALO + 2))

    def side_of(pair, g):
        return back(pair, g * GROUP + HALO - 1)

    def channel_of(s):
        return group * each + s

    def first_level(s):
        return (channel_of(s) & (levels - 1)) == 0

    def last_level(s):
        return (channel_of(s) & (levels - 1)) == levels - 1

    def level_up(c):
        return c - 1 if c % levels else c

    def level_down(c):
        return c + 1 if (c + 1) % levels else c

    def over(body, carry=0):
        for s in range(each):
            carry = body(s, carry)
        return carry

    def pack_field(value):
        south_part = (lane >= HALO) & (lane < 2 * HALO)
        north_part = (lane >= 2 * HALO) & (lane < 3 * HALO)
        picked = jnp.where(south_part, roll_lanes(value, HALO), jnp.where(north_part, roll_lanes(value, 3 * HALO), 0.0))
        return everywhere(picked)

    outer = (slice(0, SUB), slice(2 * SUB, 3 * SUB))

    def both(ref):
        return jnp.where(sub < HALO, ref[outer[1], :], ref[outer[0], :])

    def fetch(ref, rows):
        return both(ref) if rows is outer else ref[rows, :]

    def place_at(ref, rows, value):
        for part in rows if rows is outer else (rows,):
            ref[part, :] = value

    def pack_strip(ref, s, rows):
        packed = zero
        for g in range(GROUPS):
            moved = roll_lanes(fetch(ref.at[g * each + s], rows), (g * GROUP + 2 * HALO) % LANE)
            packed = jnp.where(group == g, moved, packed)
        return packed

    lower_half, upper_half = pl.ds(0, HALO), pl.ds(HALO, HALO)
    before, after = pl.ds(HALO, HALO), pl.ds(4 * HALO, HALO)

    def send_strips(which, ref, hold=None):
        def body(q, carry):
            a, b = pack_strip(ref, 2 * q, own), pack_strip(ref, 2 * q + 1, own)
            if hold is not None:
                hold[2 * q + 1, own, :], hold[2 * q + 2, own, :] = a, b
            zq[which, q] = jnp.where(half, back(a, HALO), roll_lanes(b, HALO))
            return carry

        lax.fori_loop(0, each // 2, body, 0, unroll=True)
        copies = []
        for side, other in enumerate((north, south)):
            for source, target, device in (
                (pl.ds(0, SUB), pl.ds(SUB, SUB), {"gy": other}),
                (upper_half, before, {"gx": east, "gy": other}),
                (lower_half, after, {"gx": west, "gy": other}),
            ):
                copies.append(send(zq.at[which, :, source], zl.at[which, side, :, target], device))
        return copies

    def merge(which, s, rows, packed):
        q, odd = s // 2, s % 2
        from_south, from_north = fetch(zl.at[which, 0, q], rows), fetch(zl.at[which, 1, q], rows)
        if odd:
            from_south = back(from_south, GROUP // 2)
        else:
            from_north = roll_lanes(from_north, GROUP // 2)
        mid = jnp.where(half, back(packed, HALO), roll_lanes(packed, HALO))
        value = jnp.where(low, from_south, jnp.where(high, from_north, mid))
        return jnp.where(inside, value, 0.0)

    def build_strips(which, ref, put):
        for s in range(each):
            for g in blocks:
                rows = slice(g, g + SUB)
                put(s, rows, merge(which, s, rows, pack_strip(ref, s, rows)))

    def send_rows(ref, out, into, width, to_east, to_west):
        count = channels * width // SUB
        place_of = lax.div(sub, width)
        for side, start in enumerate((to_east, to_west)):
            def body(k, carry):
                value = zero
                for j in range(SUB // width):
                    rows = slice(start - width * j, start - width * j + SUB)
                    value = jnp.where(place_of == j, ref[k + j * count, rows, :], value)
                out[side, k] = value
                return carry

            lax.fori_loop(0, count, body, 0, unroll=4)
        return [send(out.at[0], into.at[0], {"gx": east}), send(out.at[1], into.at[1], {"gx": west})]

    def take_rows(ref, into, width, from_west, from_east):
        count = channels * width // SUB

        def body(k, carry):
            for side, (base, offset) in enumerate(((0, from_west), (2 * SUB, from_east - 2 * SUB))):
                value = into[side, k]
                rows = slice(base, base + SUB)
                mask = (sub >= offset) & (sub < offset + width)
                for j in range(SUB // width):
                    shift = (offset - width * j) % SUB
                    c = k + j * count
                    ref[c, rows, :] = jnp.where(mask, roll_rows(value, shift) if shift else value, ref[c, rows, :])
            return carry

        lax.fori_loop(0, count, body, 0, unroll=4)

    def send_direct(ref):
        return [
            send(ref.at[:, pl.ds(3 * HALO, HALO)], ref.at[:, pl.ds(HALO, HALO)], {"gx": east}),
            send(ref.at[:, pl.ds(2 * HALO, HALO)], ref.at[:, pl.ds(4 * HALO, HALO)], {"gx": west}),
        ]

    def send_fields(first, values):
        for k, value in enumerate(values):
            em[first + k, own, :] = value
            es[first + k] = pack_field(value)
        which = pl.ds(first, len(values))
        copies = [
            send(em.at[which, pl.ds(3 * HALO, HALO)], em.at[which, before], {"gx": east}),
            send(em.at[which, pl.ds(2 * HALO, HALO)], em.at[which, after], {"gx": west}),
        ]
        for side, other in enumerate((north, south)):
            copies.append(send(es.at[which], el.at[side, which, pl.ds(SUB, SUB)], {"gy": other}))
            copies.append(send(es.at[which, upper_half], el.at[side, which, before], {"gx": east, "gy": other}))
            copies.append(send(es.at[which, lower_half], el.at[side, which, after], {"gx": west, "gy": other}))
        return copies

    def take_field(k, target):
        for r in range(0, 3 * SUB, SUB):
            rows = slice(r, r + SUB)
            value = em[k, rows, :]
            piece = jnp.where(
                low, back(el[0, k, rows, :], GROUP // 2),
                jnp.where(high, roll_lanes(el[1, k, rows, :], GROUP // 2), pack_field(value)),
            )
            target[0, rows, :] = value
            target[1, rows, :] = jnp.where(inside, piece, 0.0)

    def along(field, g, shift):
        return field[0, g + shift:g + shift + SUB, :], field[1, g + shift:g + shift + SUB, :]

    def latitude(main, piece):
        side = side_of(edges(piece, piece), 0)
        h_n = jnp.where(last_lane, side, back(main, 1))
        h_s = jnp.where(first_lane, side, roll_lanes(main, 1))
        return h_n, h_s, back(piece, 1), roll_lanes(piece, 1)

    def total_of(step, rows):
        main = state[step, 0, rows, :]
        for c in range(1, levels):
            main = main + state[step, c, rows, :]
        piece = zero
        for s in range(each):
            piece = piece + jnp.where(channel_of(s) < levels, strip[step, s + 1, rows, :], 0.0)
        return main, everywhere(piece)

    def slopes(step, advance):
        for g in blocks:
            rows = slice(g, g + SUB)
            main, piece = along(hf.at[step], g, 0)
            main_e, piece_e = along(hf.at[step], g, 1)
            main_w, piece_w = along(hf.at[step], g, -1)
            main_n, main_s, piece_n, piece_s = latitude(main, piece)
            af[step, 0, rows, :] = (-0.25 * ADVECTION) * (main_n - main_s)
            af[step, 1, rows, :] = (-0.25 * ADVECTION) * (piece_n - piece_s)
            bf[step, 0, rows, :] = (0.25 * ADVECTION) * (main_e - main_w)
            bf[step, 1, rows, :] = (0.25 * ADVECTION) * (piece_e - piece_w)
            if not advance:
                continue
            totals = total_of(step, rows)
            for k, (h, h_e, h_w, h_n, h_s) in enumerate((
                (main, main_e, main_w, main_n, main_s), (piece, piece_e, piece_w, piece_n, piece_s),
            )):
                lap = h_e + h_w + h_n + h_s - 4.0 * h
                value = h + HEIGHT_DIFFUSION * lap - HEIGHT_DAMPING * jnp.tanh(h)
                value = value + (BUOYANCY / levels) * wf[k, rows, :] * totals[k]
                hf[step + 1, k, rows, :] = jnp.where(inside, value, 0.0) if k else value

    def wrap_strips(ref):
        for g in blocks:
            rows = slice(g, g + SUB)
            ref[0, rows, :] = roll_lanes(ref[each, rows, :], GROUP)
            ref[each + 1, rows, :] = back(ref[1, rows, :], GROUP)

    def strip_vertical(ref, s, rows, value):
        upper = jnp.where(first_level(s), value, ref[s, rows, :])
        lower = jnp.where(last_level(s), value, ref[s + 2, rows, :])
        return upper + lower - 2.0 * value

    for load in loads[1:]:
        load.wait()
    fields_a = send_fields(0, (height_ref[...], mask_ref[...].astype(jnp.float32), hw_ref[...]))

    for s in range(each):
        value = zero
        for g in range(GROUPS):
            c = g * each + s
            value = jnp.where(group == g, diff_ref[c // levels, c % levels], value)
        sdiff[s] = value
    for step in range(1, ITERS):
        for k in range(2):
            hf[step, k, 0:SUB, :] = zero
            hf[step, k, 2 * SUB:3 * SUB, :] = zero
    for k in range(2):
        for r in range(0, 3 * SUB, SUB):
            gu[k, r:r + SUB, :] = zero
            gv[k, r:r + SUB, :] = zero

    weight_edges = send_strips(1, lam)
    for copy in a2a:
        copy.wait_recv()
    first = state.at[0]
    for p in range(n):
        holder = holder_ref[0, 0, p]
        if piece_rows % SUB == 0:
            depth = piece_rows // SUB
            for c in range(depth):
                first[p * depth + c, own, :] = recv[holder, c * SUB:(c + 1) * SUB, :]
        else:
            for r in range(piece_rows):
                row = p * piece_rows + r
                at = SUB + row % SUB
                first[row // SUB, at:at + 1, :] = recv[holder, r:r + 1, :]

    start_copies = send_direct(first)
    edge_copies = send_strips(0, first, strip.at[0])
    weight_copies = send_direct(lam) + weight_edges

    wait_all(fields_a)
    take_field(0, hf.at[0])
    take_field(1, wf)
    take_field(2, lh)

    def put_first(s, rows, value):
        place_at(strip.at[0, s + 1], rows, value)
        place_at(pairs.at[s], rows, edges(value, value))

    def roll_pass(step, s, rows):
        pair = fetch(pairs.at[s], rows)
        for g in range(GROUPS):
            c = g * each + s
            value = fetch(state.at[step, c], rows)
            side = side_of(pair, g)
            c_s = jnp.where(first_lane, side, roll_lanes(value, 1))
            c_n = jnp.where(last_lane, side, back(value, 1))
            place_at(dy.at[step, c], rows, c_n - c_s)
            place_at(mu.at[c], rows, c_n + c_s)
        value = fetch(strip.at[step, s + 1], rows)
        c_s, c_n = roll_lanes(value, 1), back(value, 1)
        place_at(sdy.at[step, s], rows, c_n - c_s)
        place_at(smu.at[s], rows, c_n + c_s)

    def inner_rolls(s, carry):
        roll_pass(0, s, own)
        return carry

    def outer_rolls(s, carry):
        roll_pass(0, s, outer)
        return carry

    wait_all(edge_copies[0::3])
    for s in range(each):
        put_first(s, own, merge(0, s, own, strip[0, s + 1, own, :]))
    lax.fori_loop(0, each, inner_rolls, 0, unroll=3)
    wait_all(edge_copies[1::3] + edge_copies[2::3])
    wait_all(start_copies)
    for s in range(each):
        put_first(s, outer, merge(0, s, outer, pack_strip(first, s, outer)))
    lax.fori_loop(0, each, outer_rolls, 0, unroll=3)
    wrap_strips(strip.at[0])

    def forward(step):
        def roll_body(s, carry):
            for r in blocks:
                roll_pass(step, s, slice(r, r + SUB))
            return carry

        if step:
            lax.fori_loop(0, each, roll_body, 0, unroll=3)
        for s in range(each):
            for r in blocks:
                rows, rows_e, rows_w = (slice(r + d, r + d + SUB) for d in (0, 1, -1))
                a, b, w = af[step, 0, rows, :], bf[step, 0, rows, :], wf[0, rows, :]
                for g in range(GROUPS):
                    c = g * each + s
                    value = state[step, c, rows, :]
                    c_e, c_w = state[step, c, rows_e, :], state[step, c, rows_w, :]
                    levels_sum = state[step, level_up(c), rows, :] + state[step, level_down(c), rows, :]
                    d = diff_ref[c // levels, c % levels]
                    change = d * (c_e + c_w + mu[c, rows, :]) + VERTICAL_MIX * levels_sum
                    change = change - (4.0 * d + 2.0 * VERTICAL_MIX) * value
                    state[step + 1, c, rows, :] = value + w * (change - a * (c_e - c_w) - b * dy[step, c, rows, :])
                a, b, w = af[step, 1, rows, :], bf[step, 1, rows, :], wf[1, rows, :]
                value = strip[step, s + 1, rows, :]
                c_e, c_w = strip[step, s + 1, rows_e, :], strip[step, s + 1, rows_w, :]
                lap = c_e + c_w + smu[s, rows, :] - 4.0 * value
                vert = strip_vertical(strip.at[step], s, rows, value)
                value = value + w * (sdiff[s] * lap - a * (c_e - c_w) - b * sdy[step, s, rows, :] + VERTICAL_MIX * vert)
                strip[step + 1, s + 1, rows, :] = value
                pairs[s, rows, :] = edges(value, value)

    outer_copies, fields_b = [], []
    for step in range(ITERS - 1):
        slopes(step, True)
        if step == 1:
            pass
        forward(step)
        if step == 1:
            outer_copies = send_rows(state.at[2], ys, yr, 2, 3 * HALO, 2 * HALO + 2)
            outer_copies += send_strips(2, state.at[2])
        if step < 2:
            wrap_strips(strip.at[step + 1])
    slopes(3, False)

    def last_sums(s, carry):
        total_u, total_v = carry
        pair = pairs[s, own, :]
        for g in range(GROUPS):
            c = g * each + s
            value = state[3, c, own, :]
            side = side_of(pair, g)
            m = wf[0, own, :] * lam[c, own, :]
            delta = jnp.where(last_lane, side, back(value, 1)) - jnp.where(first_lane, side, roll_lanes(value, 1))
            total_u = total_u + m * (state[3, c, SUB + 1:2 * SUB + 1, :] - state[3, c, SUB - 1:2 * SUB - 1, :])
            total_v = total_v + m * delta
        return total_u, total_v

    total_u, total_v = over(last_sums, (zero, zero))
    fields_c = send_fields(3, (hf[2, 0, own, :], total_u, total_v, hf[3, 0, own, :]))

    def put_weight(s, rows, value):
        slam[s, rows, :] = value

    wait_all(weight_copies)
    build_strips(1, lam, put_weight)

    def spread_pair(step, s, rows, m):
        bm = bf[step, 1, rows, :] * m
        dm = sdiff[s] * m
        pairs[s, rows, :] = edges(dm - bm, dm + bm)

    def put_outer(s, rows, value):
        sdy[2, s, rows, :] = back(value, 1) - roll_lanes(value, 1)
        strip[2, s + 1, rows, :] = value
        pairs[s, rows, :] = edges(value, value)

    wait_all(outer_copies)
    take_rows(state.at[2], yr, 2, HALO, 2 * SUB + 2)
    build_strips(2, state.at[2], put_outer)

    def outer_slopes(s, carry):
        for r in blocks:
            rows = slice(r, r + SUB)
            pair = pairs[s, rows, :]
            for g in range(GROUPS):
                c = g * each + s
                value = state[2, c, rows, :]
                side = side_of(pair, g)
                dy[2, c, rows, :] = (
                    jnp.where(last_lane, side, back(value, 1)) - jnp.where(first_lane, side, roll_lanes(value, 1))
                )
        return carry

    over(outer_slopes)
    def weigh(s, carry):
        for r in blocks:
            rows = slice(r, r + SUB)
            for g in range(GROUPS):
                c = g * each + s
                mu[c, rows, :] = wf[0, rows, :] * lam[c, rows, :]
            smu[s + 1, rows, :] = wf[1, rows, :] * slam[s, rows, :]
        return carry

    over(weigh)
    wrap_strips(smu)
    wait_all(fields_c)
    take_field(3, hf.at[2])
    slopes(2, False)
    take_field(4, gu)
    take_field(5, gv)
    take_field(6, hf.at[3])
    slopes(3, False)
    for copy in a2a + sends:
        copy.wait_send()

    def sums(step):
        def body(s, carry):
            result = []
            for r, (total_u, total_v, strip_u, strip_v) in zip(blocks, (carry[:4], carry[4:])):
                rows, rows_e, rows_w = (slice(r + d, r + d + SUB) for d in (0, 1, -1))
                w = wf[0, rows, :]
                for g in range(GROUPS):
                    c = g * each + s
                    m = w * lam[c, rows, :]
                    mu[c, rows, :] = m
                    total_u = total_u + m * (state[step, c, rows_e, :] - state[step, c, rows_w, :])
                    total_v = total_v + m * dy[step, c, rows, :]
                m = wf[1, rows, :] * slam[s, rows, :]
                smu[s + 1, rows, :] = m
                strip_u = strip_u + m * (strip[step, s + 1, rows_e, :] - strip[step, s + 1, rows_w, :])
                strip_v = strip_v + m * sdy[step, s, rows, :]
                spread_pair(step, s, rows, m)
                result += [total_u, total_v, strip_u, strip_v]
            return tuple(result)

        totals = over(body, (zero,) * 8)
        for r, (total_u, total_v, strip_u, strip_v) in zip(blocks, (totals[:4], totals[4:])):
            rows = slice(r, r + SUB)
            gu[0, rows, :], gv[0, rows, :] = total_u, total_v
            gu[1, rows, :], gv[1, rows, :] = everywhere(strip_u), everywhere(strip_v)

    def adjoint(step):
        last = step == 0

        def body(s, carry):
            for r in (SUB,) if last else blocks:
                rows, rows_e, rows_w = (slice(r + d, r + d + SUB) for d in (0, 1, -1))
                pair = pairs[s, rows, :]
                a_e, a_w, b = af[step, 0, rows_e, :], af[step, 0, rows_w, :], bf[step, 0, rows, :]
                push = prow[0, rows, :]
                for g in range(GROUPS):
                    c = g * each + s
                    m = mu[c, rows, :]
                    m_e, m_w = mu[c, rows_e, :], mu[c, rows_w, :]
                    vert = mu[level_up(c), rows, :] + mu[level_down(c), rows, :] - 2.0 * m
                    d = diff_ref[c // levels, c % levels]
                    bm = b * m
                    dm = d * m
                    side = side_of(pair, g)
                    from_s = jnp.where(first_lane, side, roll_lanes(dm - bm, 1))
                    from_n = jnp.where(last_lane, side, back(dm + bm, 1))
                    value = lam[c, rows, :] + VERTICAL_MIX * vert - 4.0 * dm + from_s + from_n
                    value = value + d * (m_w + m_e) + (a_e * m_e - a_w * m_w)
                    if c < levels:
                        value = value + push
                    if last:
                        out_ref[c] = value
                    else:
                        lam[c, rows, :] = value
                if last:
                    continue
                m, m_e, m_w = smu[s + 1, rows, :], smu[s + 1, rows_e, :], smu[s + 1, rows_w, :]
                bm = bf[step, 1, rows, :] * m
                dm = sdiff[s] * m
                value = slam[s, rows, :] + VERTICAL_MIX * strip_vertical(smu, s, rows, m) - 4.0 * dm
                value = value + roll_lanes(dm - bm, 1) + back(dm + bm, 1) + sdiff[s] * (m_w + m_e)
                value = value + (af[step, 1, rows_e, :] * m_e - af[step, 1, rows_w, :] * m_w)
                slam[s, rows, :] = value + jnp.where(channel_of(s) < levels, prow[1, rows, :], 0.0)
            return carry

        over(body)

    for step in reversed(range(ITERS)):
        if step == ITERS - 1:
            for s in range(each):
                for r in blocks:
                    rows = slice(r, r + SUB)
                    spread_pair(3, s, rows, smu[s + 1, rows, :])
        else:
            sums(step)
            wrap_strips(smu)
        results = []
        for g in blocks:
            rows = slice(g, g + SUB)
            parts = []
            for k in range(2):
                value = lh[k, rows, :]
                prow[k, rows, :] = (BUOYANCY / levels) * wf[k, rows, :] * value
                turn = (0.25 * ADVECTION) * gu[k, rows, :]
                spread = HEIGHT_DIFFUSION * value
                damp = jnp.tanh(hf[step, k, rows, :])
                kept = value - 4.0 * spread - HEIGHT_DAMPING * (1.0 - damp * damp) * value
                before, after = slice(g - 1, g - 1 + SUB), slice(g + 1, g + 1 + SUB)
                kept = kept + HEIGHT_DIFFUSION * (lh[k, before, :] + lh[k, after, :])
                kept = kept + (0.25 * ADVECTION) * (gv[k, after, :] - gv[k, before, :])
                parts.append((kept, spread + turn, spread - turn))
            (main, to_n, to_s), (piece, piece_n, piece_s) = parts
            side = side_of(edges(piece_n, piece_s), 0)
            main = main + jnp.where(first_lane, side, roll_lanes(to_n, 1)) + jnp.where(last_lane, side, back(to_s, 1))
            piece = piece + roll_lanes(piece_n, 1) + back(piece_s, 1)
            results.append((main, jnp.where(inside, piece, 0.0)))
        for g, result in zip(blocks, results):
            for k in range(2):
                lh[k, g:g + SUB, :] = result[k]
        adjoint(step)

    outh_ref[...] = lh[0, own, :]


def local(checkpoint, holder_list, height, land_mask, diffusivity, tracer_weight, height_weight):
    n, n_y = lax.axis_size("gx"), lax.axis_size("gy")
    width_x, width_y = height.shape
    assert (width_x, width_y) == (SUB, LANE)
    levels = diffusivity.shape[1]
    channels = 3 * levels
    each = channels // GROUPS
    piece_rows = checkpoint.shape[3] // LANE
    padded = -(-piece_rows // SUB) * SUB
    f32 = jnp.float32
    vmem = pl.BlockSpec(memory_space=pltpu.VMEM)
    tile = pltpu.VMEM((SUB, LANE), f32)
    field = pltpu.VMEM((2, 3 * SUB, LANE), f32)
    fields = pltpu.VMEM((ITERS, 2, 3 * SUB, LANE), f32)
    volume = pltpu.VMEM((channels, 3 * SUB, LANE), f32)

    def strips(*lead):
        return pltpu.VMEM((*lead, 3 * SUB, LANE), f32)

    half = channels * HALO // SUB
    out, out_h = pl.pallas_call(
        functools.partial(kernel, n, n_y, levels, piece_rows),
        out_shape=(pltpu.VMEM((channels, SUB, LANE), f32), pltpu.VMEM((SUB, LANE), f32)),
        in_specs=[pl.BlockSpec(memory_space=pltpu.HBM)] * 7,
        out_specs=(vmem, vmem),
        scratch_shapes=[
            pltpu.VMEM((n * padded, LANE), f32),
            pltpu.VMEM((n, padded, LANE), f32),
            pltpu.VMEM((ITERS, channels, 3 * SUB, LANE), f32),
            strips(ITERS, each + 2),
            volume, strips(each),
            volume, strips(each + 2),
            pltpu.VMEM((3, channels, 3 * SUB, LANE), f32), strips(3, each),
            strips(each),
            pltpu.VMEM((each, SUB, LANE), f32),
            fields, fields, fields,
            field, field, field, field, field,
            strips(8),
            pltpu.VMEM((8, SUB, LANE), f32),
            strips(2, 8),
            pltpu.VMEM((3, each // 2, SUB, LANE), f32),
            strips(3, 2, each // 2),
            pltpu.VMEM((2, 2, half, SUB, LANE), f32),
            pltpu.VMEM((2, 2, half, SUB, LANE), f32),
            pltpu.VMEM((2, half // 2, SUB, LANE), f32),
            pltpu.VMEM((2, half // 2, SUB, LANE), f32),
            pltpu.SMEM(holder_list.shape, jnp.int32),
            pltpu.SMEM(diffusivity.shape, f32),
            pltpu.VMEM(checkpoint.shape[2:], f32),
            tile,
            pltpu.VMEM((SUB, LANE), jnp.int32),
            tile,
            pltpu.SemaphoreType.DMA((n,)),
            pltpu.SemaphoreType.DMA((n,)),
            pltpu.SemaphoreType.DMA((48,)),
            pltpu.SemaphoreType.DMA((48,)),
            pltpu.SemaphoreType.DMA((7,)),
        ],
        compiler_params=pltpu.CompilerParams(
            collective_id=0, has_side_effects=True, vmem_limit_bytes=60 * 2**20
        ),
    )(
        holder_list, diffusivity, checkpoint.reshape(checkpoint.shape[2:]), height, land_mask,
        tracer_weight.reshape(channels, SUB, LANE), height_weight,
    )
    return out.reshape(tracer_weight.shape), out_h


def solution(mesh):
    return jax.shard_map(
        local,
        mesh=mesh,
        in_specs=(
            P(("member", "gx"), "gy", None, None),
            P(("member", "gx"), "gy", None),
            P(("member", "gx"), "gy"),
            P("gx", "gy"),
            P(),
            P("member", None, "gx", "gy"),
            P(("member", "gx"), "gy"),
        ),
        out_specs=(P("member", None, "gx", "gy"), P(("member", "gx"), "gy")),
        check_vma=False,
    )
```

```python
import functools
import jax
import jax.numpy as jnp
from jax import lax
from jax.experimental import pallas as pl
from jax.experimental.pallas import tpu as pltpu
from jax.sharding import PartitionSpec as P

ITERS = 4
ADVECTION = 0.3
VERTICAL_MIX = 0.1
HEIGHT_DIFFUSION = 0.2
HEIGHT_DAMPING = 0.3
BUOYANCY = 0.5

SUB = 8
LANE = 128
HALO = 4
GROUP = 16
GROUPS = LANE // GROUP
MESH = pl.DeviceIdType.MESH


def roll_lanes(value, shift):
    return pltpu.roll(value, shift, 1)


def roll_rows(value, shift):
    return pltpu.roll(value, shift, 0)


def kernel(
    n, n_y, levels, piece_rows,
    holder_hbm, diff_hbm, ckpt_hbm, height_hbm, mask_hbm, tw_hbm, hw_hbm,
    out_ref, outh_ref,
    buf, recv, state, strip, lam, slam, mu, smu, dy, sdy, pairs, sdiff,
    hf, af, bf, wf, lh, gu, gv, prow,
    em, es, el, zq, zl, xs, xr, ys, yr,
    holder_ref, diff_ref, ckpt_ref, height_ref, mask_ref, hw_ref,
    a2a_send, a2a_recv, send_sem, recv_sem, in_sem,
):
    me = lax.axis_index("gx")
    my = lax.axis_index("gy")
    east, west = lax.rem(me + 1, n), lax.rem(me + n - 1, n)
    north, south = lax.rem(my + 1, n_y), lax.rem(my + n_y - 1, n_y)
    channels = 3 * levels
    each = channels // GROUPS
    padded = -(-piece_rows // SUB) * SUB
    own = slice(SUB, 2 * SUB)
    blocks = (HALO, HALO + SUB)

    inputs = (
        (ckpt_hbm, ckpt_ref), (diff_hbm, diff_ref), (mask_hbm, mask_ref), (tw_hbm, lam.at[:, pl.ds(SUB, SUB)]),
        (height_hbm, height_ref), (hw_hbm, hw_ref), (holder_hbm, holder_ref),
    )
    loads = [pltpu.make_async_copy(source, target, in_sem.at[i]) for i, (source, target) in enumerate(inputs)]
    for load in loads:
        load.start()

    barrier = pltpu.get_barrier_semaphore()
    for k in range(1, n):
        pl.semaphore_signal(barrier, inc=1, device_id={"gx": lax.rem(me + k, n)}, device_id_type=MESH)
    for other in (north, south):
        pl.semaphore_signal(barrier, inc=1, device_id={"gy": other}, device_id_type=MESH)
        for side in (east, west):
            pl.semaphore_signal(barrier, inc=1, device_id={"gx": side, "gy": other}, device_id_type=MESH)

    loads[0].wait()
    if padded != piece_rows:
        buf[...] = jnp.zeros_like(buf)
    for o in range(0, n, SUB):
        size = min(SUB, n - o)
        for r in range(piece_rows):
            buf[pl.ds(o * padded + r, size, stride=padded), :] = ckpt_ref[o:o + size, r * LANE:(r + 1) * LANE]

    pl.semaphore_wait(barrier, n + 5)

    mine = pl.multiple_of(me * padded, SUB)
    sends = []
    a2a = []
    for k in range(1, n):
        owner = lax.rem(me + k, n)
        copy = pltpu.make_async_remote_copy(
            src_ref=buf.at[pl.ds(pl.multiple_of(owner * padded, SUB), padded)],
            dst_ref=recv.at[me],
            send_sem=a2a_send.at[k], recv_sem=a2a_recv.at[k],
            device_id={"gx": owner}, device_id_type=MESH,
        )
        copy.start()
        a2a.append(copy)
    recv[me] = buf[pl.ds(mine, padded), :]

    used = [0]

    def send(source, target, device):
        i = used[0]
        used[0] += 1
        copy = pltpu.make_async_remote_copy(
            src_ref=source, dst_ref=target, send_sem=send_sem.at[i], recv_sem=recv_sem.at[i],
            device_id=device, device_id_type=MESH,
        )
        copy.start()
        sends.append(copy)
        return copy

    def wait_all(copies):
        for copy in copies:
            copy.wait_recv()

    lane = lax.broadcasted_iota(jnp.int32, (SUB, LANE), 1)
    sub = lax.broadcasted_iota(jnp.int32, (SUB, LANE), 0)
    first_lane, last_lane = lane == 0, lane == LANE - 1
    group = lax.shift_right_logical(lane, 4)
    place = lane & (GROUP - 1)
    low, high = place < HALO, place >= GROUP - HALO
    half = place < GROUP // 2
    edge = place == HALO - 1
    below, above = jnp.where(low, my, 1), jnp.where(high, n_y - 1 - my, 1)
    inside = (below > 0) & (above > 0)
    zero = jnp.zeros((SUB, LANE), jnp.float32)

    def back(value, shift):
        return roll_lanes(value, (LANE - shift) % LANE)

    def everywhere(value):
        moved = [value] + [roll_lanes(value, GROUP * k) for k in range(1, GROUPS)]
        while len(moved) > 1:
            moved = [a + b for a, b in zip(moved[::2], moved[1::2])]
        return moved[0]

    def edges(from_south, from_north):
        return jnp.where(edge, from_south, back(from_north, GROUP - 2 * HALO + 2))

    def side_of(pair, g):
        return back(pair, g * GROUP + HALO - 1)

    def channel_of(s):
        return group * each + s

    def first_level(s):
        return (channel_of(s) & (levels - 1)) == 0

    def last_level(s):
        return (channel_of(s) & (levels - 1)) == levels - 1

    def level_up(c):
        return c - 1 if c % levels else c

    def level_down(c):
        return c + 1 if (c + 1) % levels else c

    def over(body, carry=0):
        for s in range(each):
            carry = body(s, carry)
        return carry

    def pack_field(value):
        south_part = (lane >= HALO) & (lane < 2 * HALO)
        north_part = (lane >= 2 * HALO) & (lane < 3 * HALO)
        picked = jnp.where(south_part, roll_lanes(value, HALO), jnp.where(north_part, roll_lanes(value, 3 * HALO), 0.0))
        return everywhere(picked)

    outer = (slice(0, SUB), slice(2 * SUB, 3 * SUB))

    def both(ref):
        return jnp.where(sub < HALO, ref[outer[1], :], ref[outer[0], :])

    def fetch(ref, rows):
        return both(ref) if rows is outer else ref[rows, :]

    def place_at(ref, rows, value):
        for part in rows if rows is outer else (rows,):
            ref[part, :] = value

    def pack_strip(ref, s, rows):
        packed = zero
        for g in range(GROUPS):
            moved = roll_lanes(fetch(ref.at[g * each + s], rows), (g * GROUP + 2 * HALO) % LANE)
            packed = jnp.where(group == g, moved, packed)
        return packed

    lower_half, upper_half = pl.ds(0, HALO), pl.ds(HALO, HALO)
    before, after = pl.ds(HALO, HALO), pl.ds(4 * HALO, HALO)

    def send_strips(which, ref, hold=None):
        def body(q, carry):
            a, b = pack_strip(ref, 2 * q, own), pack_strip(ref, 2 * q + 1, own)
            if hold is not None:
                hold[2 * q + 1, own, :], hold[2 * q + 2, own, :] = a, b
            zq[which, q] = jnp.where(half, back(a, HALO), roll_lanes(b, HALO))
            return carry

        lax.fori_loop(0, each // 2, body, 0, unroll=True)
        copies = []
        for side, other in enumerate((north, south)):
            for source, target, device in (
                (pl.ds(0, SUB), pl.ds(SUB, SUB), {"gy": other}),
                (upper_half, before, {"gx": east, "gy": other}),
                (lower_half, after, {"gx": west, "gy": other}),
            ):
                copies.append(send(zq.at[which, :, source], zl.at[which, side, :, target], device))
        return copies

    def merge(which, s, rows, packed):
        q, odd = s // 2, s % 2
        from_south, from_north = fetch(zl.at[which, 0, q], rows), fetch(zl.at[which, 1, q], rows)
        if odd:
            from_south = back(from_south, GROUP // 2)
        else:
            from_north = roll_lanes(from_north, GROUP // 2)
        mid = jnp.where(half, back(packed, HALO), roll_lanes(packed, HALO))
        value = jnp.where(low, from_south, jnp.where(high, from_north, mid))
        return jnp.where(inside, value, 0.0)

    def build_strips(which, ref, put):
        for s in range(each):
            for g in blocks:
                rows = slice(g, g + SUB)
                put(s, rows, merge(which, s, rows, pack_strip(ref, s, rows)))

    def send_rows(ref, out, into, width, to_east, to_west):
        count = channels * width // SUB
        place_of = lax.div(sub, width)
        for side, start in enumerate((to_east, to_west)):
            def body(k, carry):
                value = zero
                for j in range(SUB // width):
                    rows = slice(start - width * j, start - width * j + SUB)
                    value = jnp.where(place_of == j, ref[k + j * count, rows, :], value)
                out[side, k] = value
                return carry

            lax.fori_loop(0, count, body, 0, unroll=4)
        return [send(out.at[0], into.at[0], {"gx": east}), send(out.at[1], into.at[1], {"gx": west})]

    def take_rows(ref, into, width, from_west, from_east):
        count = channels * width // SUB

        def body(k, carry):
            for side, (base, offset) in enumerate(((0, from_west), (2 * SUB, from_east - 2 * SUB))):
                value = into[side, k]
                rows = slice(base, base + SUB)
                mask = (sub >= offset) & (sub < offset + width)
                for j in range(SUB // width):
                    shift = (offset - width * j) % SUB
                    c = k + j * count
                    ref[c, rows, :] = jnp.where(mask, roll_rows(value, shift) if shift else value, ref[c, rows, :])
            return carry

        lax.fori_loop(0, count, body, 0, unroll=4)

    def send_direct(ref):
        return [
            send(ref.at[:, pl.ds(3 * HALO, HALO)], ref.at[:, pl.ds(HALO, HALO)], {"gx": east}),
            send(ref.at[:, pl.ds(2 * HALO, HALO)], ref.at[:, pl.ds(4 * HALO, HALO)], {"gx": west}),
        ]

    def send_fields(first, values):
        for k, value in enumerate(values):
            em[first + k, own, :] = value
            es[first + k] = pack_field(value)
        which = pl.ds(first, len(values))
        copies = [
            send(em.at[which, pl.ds(3 * HALO, HALO)], em.at[which, before], {"gx": east}),
            send(em.at[which, pl.ds(2 * HALO, HALO)], em.at[which, after], {"gx": west}),
        ]
        for side, other in enumerate((north, south)):
            copies.append(send(es.at[which], el.at[side, which, pl.ds(SUB, SUB)], {"gy": other}))
            copies.append(send(es.at[which, upper_half], el.at[side, which, before], {"gx": east, "gy": other}))
            copies.append(send(es.at[which, lower_half], el.at[side, which, after], {"gx": west, "gy": other}))
        return copies

    def take_field(k, target):
        for r in range(0, 3 * SUB, SUB):
            rows = slice(r, r + SUB)
            value = em[k, rows, :]
            piece = jnp.where(
                low, back(el[0, k, rows, :], GROUP // 2),
                jnp.where(high, roll_lanes(el[1, k, rows, :], GROUP // 2), pack_field(value)),
            )
            target[0, rows, :] = value
            target[1, rows, :] = jnp.where(inside, piece, 0.0)

    def along(field, g, shift):
        return field[0, g + shift:g + shift + SUB, :], field[1, g + shift:g + shift + SUB, :]

    def latitude(main, piece):
        side = side_of(edges(piece, piece), 0)
        h_n = jnp.where(last_lane, side, back(main, 1))
        h_s = jnp.where(first_lane, side, roll_lanes(main, 1))
        return h_n, h_s, back(piece, 1), roll_lanes(piece, 1)

    def total_of(step, rows):
        main = state[step, 0, rows, :]
        for c in range(1, levels):
            main = main + state[step, c, rows, :]
        piece = zero
        for s in range(each):
            piece = piece + jnp.where(channel_of(s) < levels, strip[step, s + 1, rows, :], 0.0)
        return main, everywhere(piece)

    def slopes(step, advance):
        for g in blocks:
            rows = slice(g, g + SUB)
            main, piece = along(hf.at[step], g, 0)
            main_e, piece_e = along(hf.at[step], g, 1)
            main_w, piece_w = along(hf.at[step], g, -1)
            main_n, main_s, piece_n, piece_s = latitude(main, piece)
            af[step, 0, rows, :] = (-0.25 * ADVECTION) * (main_n - main_s)
            af[step, 1, rows, :] = (-0.25 * ADVECTION) * (piece_n - piece_s)
            bf[step, 0, rows, :] = (0.25 * ADVECTION) * (main_e - main_w)
            bf[step, 1, rows, :] = (0.25 * ADVECTION) * (piece_e - piece_w)
            if not advance:
                continue
            totals = total_of(step, rows)
            for k, (h, h_e, h_w, h_n, h_s) in enumerate((
                (main, main_e, main_w, main_n, main_s), (piece, piece_e, piece_w, piece_n, piece_s),
            )):
                lap = h_e + h_w + h_n + h_s - 4.0 * h
                value = h + HEIGHT_DIFFUSION * lap - HEIGHT_DAMPING * jnp.tanh(h)
                value = value + (BUOYANCY / levels) * wf[k, rows, :] * totals[k]
                hf[step + 1, k, rows, :] = jnp.where(inside, value, 0.0) if k else value

    def wrap_strips(ref):
        for g in blocks:
            rows = slice(g, g + SUB)
            ref[0, rows, :] = roll_lanes(ref[each, rows, :], GROUP)
            ref[each + 1, rows, :] = back(ref[1, rows, :], GROUP)

    def strip_vertical(ref, s, rows, value):
        upper = jnp.where(first_level(s), value, ref[s, rows, :])
        lower = jnp.where(last_level(s), value, ref[s + 2, rows, :])
        return upper + lower - 2.0 * value

    for load in loads[1:]:
        load.wait()
    fields_a = send_fields(0, (height_ref[...], mask_ref[...].astype(jnp.float32), hw_ref[...]))

    for s in range(each):
        value = zero
        for g in range(GROUPS):
            c = g * each + s
            value = jnp.where(group == g, diff_ref[c // levels, c % levels], value)
        sdiff[s] = value
    for step in range(1, ITERS):
        for k in range(2):
            hf[step, k, 0:SUB, :] = zero
            hf[step, k, 2 * SUB:3 * SUB, :] = zero
    for k in range(2):
        for r in range(0, 3 * SUB, SUB):
            gu[k, r:r + SUB, :] = zero
            gv[k, r:r + SUB, :] = zero

    weight_edges = send_strips(1, lam)
    for copy in a2a:
        copy.wait_recv()
    first = state.at[0]
    for p in range(n):
        holder = holder_ref[0, 0, p]
        if piece_rows % SUB == 0:
            depth = piece_rows // SUB
            for c in range(depth):
                first[p * depth + c, own, :] = recv[holder, c * SUB:(c + 1) * SUB, :]
        else:
            for r in range(piece_rows):
                row = p * piece_rows + r
                at = SUB + row % SUB
                first[row // SUB, at:at + 1, :] = recv[holder, r:r + 1, :]

    start_copies = send_direct(first)
    edge_copies = send_strips(0, first, strip.at[0])
    weight_copies = send_direct(lam) + weight_edges

    wait_all(fields_a)
    take_field(0, hf.at[0])
    take_field(1, wf)
    take_field(2, lh)

    def put_first(s, rows, value):
        place_at(strip.at[0, s + 1], rows, value)
        place_at(pairs.at[s], rows, edges(value, value))

    def roll_pass(step, s, rows):
        pair = fetch(pairs.at[s], rows)
        for g in range(GROUPS):
            c = g * each + s
            value = fetch(state.at[step, c], rows)
            side = side_of(pair, g)
            c_s = jnp.where(first_lane, side, roll_lanes(value, 1))
            c_n = jnp.where(last_lane, side, back(value, 1))
            place_at(dy.at[step, c], rows, c_n - c_s)
            place_at(mu.at[c], rows, c_n + c_s)
        value = fetch(strip.at[step, s + 1], rows)
        c_s, c_n = roll_lanes(value, 1), back(value, 1)
        place_at(sdy.at[step, s], rows, c_n - c_s)
        place_at(smu.at[s], rows, c_n + c_s)

    def inner_rolls(s, carry):
        roll_pass(0, s, own)
        return carry

    def outer_rolls(s, carry):
        roll_pass(0, s, outer)
        return carry

    wait_all(edge_copies[0::3])
    for s in range(each):
        put_first(s, own, merge(0, s, own, strip[0, s + 1, own, :]))
    lax.fori_loop(0, each, inner_rolls, 0, unroll=3)
    wait_all(edge_copies[1::3] + edge_copies[2::3])
    wait_all(start_copies)
    for s in range(each):
        put_first(s, outer, merge(0, s, outer, pack_strip(first, s, outer)))
    lax.fori_loop(0, each, outer_rolls, 0, unroll=3)
    wrap_strips(strip.at[0])

    def forward(step):
        def roll_body(s, carry):
            for r in blocks:
                roll_pass(step, s, slice(r, r + SUB))
            return carry

        if step:
            lax.fori_loop(0, each, roll_body, 0, unroll=3)
        for s in range(each):
            for r in blocks:
                rows, rows_e, rows_w = (slice(r + d, r + d + SUB) for d in (0, 1, -1))
                a, b, w = af[step, 0, rows, :], bf[step, 0, rows, :], wf[0, rows, :]
                for g in range(GROUPS):
                    c = g * each + s
                    value = state[step, c, rows, :]
                    c_e, c_w = state[step, c, rows_e, :], state[step, c, rows_w, :]
                    levels_sum = state[step, level_up(c), rows, :] + state[step, level_down(c), rows, :]
                    d = diff_ref[c // levels, c % levels]
                    change = d * (c_e + c_w + mu[c, rows, :]) + VERTICAL_MIX * levels_sum
                    change = change - (4.0 * d + 2.0 * VERTICAL_MIX) * value
                    state[step + 1, c, rows, :] = value + w * (change - a * (c_e - c_w) - b * dy[step, c, rows, :])
                a, b, w = af[step, 1, rows, :], bf[step, 1, rows, :], wf[1, rows, :]
                value = strip[step, s + 1, rows, :]
                c_e, c_w = strip[step, s + 1, rows_e, :], strip[step, s + 1, rows_w, :]
                lap = c_e + c_w + smu[s, rows, :] - 4.0 * value
                vert = strip_vertical(strip.at[step], s, rows, value)
                value = value + w * (sdiff[s] * lap - a * (c_e - c_w) - b * sdy[step, s, rows, :] + VERTICAL_MIX * vert)
                strip[step + 1, s + 1, rows, :] = value
                pairs[s, rows, :] = edges(value, value)

    outer_copies, fields_b = [], []
    for step in range(ITERS - 1):
        slopes(step, True)
        if step == 1:
            pass
        forward(step)
        if step == 1:
            outer_edges = send_strips(2, state.at[2])
            outer_copies = send_rows(state.at[2], ys, yr, 2, 3 * HALO, 2 * HALO + 2) + outer_edges
        if step < 2:
            wrap_strips(strip.at[step + 1])
    slopes(3, False)

    def last_sums(s, carry):
        total_u, total_v = carry
        pair = pairs[s, own, :]
        for g in range(GROUPS):
            c = g * each + s
            value = state[3, c, own, :]
            side = side_of(pair, g)
            m = wf[0, own, :] * lam[c, own, :]
            delta = jnp.where(last_lane, side, back(value, 1)) - jnp.where(first_lane, side, roll_lanes(value, 1))
            total_u = total_u + m * (state[3, c, SUB + 1:2 * SUB + 1, :] - state[3, c, SUB - 1:2 * SUB - 1, :])
            total_v = total_v + m * delta
        return total_u, total_v

    total_u, total_v = over(last_sums, (zero, zero))
    fields_c = send_fields(3, (hf[2, 0, own, :], total_u, total_v, hf[3, 0, own, :]))

    def put_weight(s, rows, value):
        slam[s, rows, :] = value

    wait_all(weight_copies)
    build_strips(1, lam, put_weight)

    def spread_pair(step, s, rows, m):
        bm = bf[step, 1, rows, :] * m
        dm = sdiff[s] * m
        pairs[s, rows, :] = edges(dm - bm, dm + bm)

    def put_outer(s, rows, value):
        sdy[2, s, rows, :] = back(value, 1) - roll_lanes(value, 1)
        strip[2, s + 1, rows, :] = value
        pairs[s, rows, :] = edges(value, value)

    wait_all(outer_copies)
    take_rows(state.at[2], yr, 2, HALO, 2 * SUB + 2)
    build_strips(2, state.at[2], put_outer)

    def outer_slopes(s, carry):
        for r in blocks:
            rows = slice(r, r + SUB)
            pair = pairs[s, rows, :]
            for g in range(GROUPS):
                c = g * each + s
                value = state[2, c, rows, :]
                side = side_of(pair, g)
                dy[2, c, rows, :] = (
                    jnp.where(last_lane, side, back(value, 1)) - jnp.where(first_lane, side, roll_lanes(value, 1))
                )
        return carry

    over(outer_slopes)
    def weigh(s, carry):
        for r in blocks:
            rows = slice(r, r + SUB)
            for g in range(GROUPS):
                c = g * each + s
                mu[c, rows, :] = wf[0, rows, :] * lam[c, rows, :]
            smu[s + 1, rows, :] = wf[1, rows, :] * slam[s, rows, :]
        return carry

    over(weigh)
    wrap_strips(smu)
    wait_all(fields_c)
    take_field(3, hf.at[2])
    slopes(2, False)
    take_field(4, gu)
    take_field(5, gv)
    take_field(6, hf.at[3])
    slopes(3, False)
    for copy in a2a + sends:
        copy.wait_send()

    def sums(step):
        def body(s, carry):
            result = []
            for r, (total_u, total_v, strip_u, strip_v) in zip(blocks, (carry[:4], carry[4:])):
                rows, rows_e, rows_w = (slice(r + d, r + d + SUB) for d in (0, 1, -1))
                w = wf[0, rows, :]
                for g in range(GROUPS):
                    c = g * each + s
                    m = w * lam[c, rows, :]
                    mu[c, rows, :] = m
                    total_u = total_u + m * (state[step, c, rows_e, :] - state[step, c, rows_w, :])
                    total_v = total_v + m * dy[step, c, rows, :]
                m = wf[1, rows, :] * slam[s, rows, :]
                smu[s + 1, rows, :] = m
                strip_u = strip_u + m * (strip[step, s + 1, rows_e, :] - strip[step, s + 1, rows_w, :])
                strip_v = strip_v + m * sdy[step, s, rows, :]
                spread_pair(step, s, rows, m)
                result += [total_u, total_v, strip_u, strip_v]
            return tuple(result)

        totals = over(body, (zero,) * 8)
        for r, (total_u, total_v, strip_u, strip_v) in zip(blocks, (totals[:4], totals[4:])):
            rows = slice(r, r + SUB)
            gu[0, rows, :], gv[0, rows, :] = total_u, total_v
            gu[1, rows, :], gv[1, rows, :] = everywhere(strip_u), everywhere(strip_v)

    def adjoint(step):
        last = step == 0

        def body(s, carry):
            for r in (SUB,) if last else blocks:
                rows, rows_e, rows_w = (slice(r + d, r + d + SUB) for d in (0, 1, -1))
                pair = pairs[s, rows, :]
                a_e, a_w, b = af[step, 0, rows_e, :], af[step, 0, rows_w, :], bf[step, 0, rows, :]
                push = prow[0, rows, :]
                for g in range(GROUPS):
                    c = g * each + s
                    m = mu[c, rows, :]
                    m_e, m_w = mu[c, rows_e, :], mu[c, rows_w, :]
                    vert = mu[level_up(c), rows, :] + mu[level_down(c), rows, :] - 2.0 * m
                    d = diff_ref[c // levels, c % levels]
                    bm = b * m
                    dm = d * m
                    side = side_of(pair, g)
                    from_s = jnp.where(first_lane, side, roll_lanes(dm - bm, 1))
                    from_n = jnp.where(last_lane, side, back(dm + bm, 1))
                    value = lam[c, rows, :] + VERTICAL_MIX * vert - 4.0 * dm + from_s + from_n
                    value = value + d * (m_w + m_e) + (a_e * m_e - a_w * m_w)
                    if c < levels:
                        value = value + push
                    if last:
                        out_ref[c] = value
                    else:
                        lam[c, rows, :] = value
                if last:
                    continue
                m, m_e, m_w = smu[s + 1, rows, :], smu[s + 1, rows_e, :], smu[s + 1, rows_w, :]
                bm = bf[step, 1, rows, :] * m
                dm = sdiff[s] * m
                value = slam[s, rows, :] + VERTICAL_MIX * strip_vertical(smu, s, rows, m) - 4.0 * dm
                value = value + roll_lanes(dm - bm, 1) + back(dm + bm, 1) + sdiff[s] * (m_w + m_e)
                value = value + (af[step, 1, rows_e, :] * m_e - af[step, 1, rows_w, :] * m_w)
                slam[s, rows, :] = value + jnp.where(channel_of(s) < levels, prow[1, rows, :], 0.0)
            return carry

        for start in range(0, each, 3):
            @pl.when(me >= 0)
            def _(start=start):
                for s in range(start, start + 3):
                    body(s, 0)

    for step in reversed(range(ITERS)):
        if step == ITERS - 1:
            for s in range(each):
                for r in blocks:
                    rows = slice(r, r + SUB)
                    spread_pair(3, s, rows, smu[s + 1, rows, :])
        else:
            sums(step)
            wrap_strips(smu)
        results = []
        for g in blocks:
            rows = slice(g, g + SUB)
            parts = []
            for k in range(2):
                value = lh[k, rows, :]
                prow[k, rows, :] = (BUOYANCY / levels) * wf[k, rows, :] * value
                turn = (0.25 * ADVECTION) * gu[k, rows, :]
                spread = HEIGHT_DIFFUSION * value
                damp = jnp.tanh(hf[step, k, rows, :])
                kept = value - 4.0 * spread - HEIGHT_DAMPING * (1.0 - damp * damp) * value
                before, after = slice(g - 1, g - 1 + SUB), slice(g + 1, g + 1 + SUB)
                kept = kept + HEIGHT_DIFFUSION * (lh[k, before, :] + lh[k, after, :])
                kept = kept + (0.25 * ADVECTION) * (gv[k, after, :] - gv[k, before, :])
                parts.append((kept, spread + turn, spread - turn))
            (main, to_n, to_s), (piece, piece_n, piece_s) = parts
            side = side_of(edges(piece_n, piece_s), 0)
            main = main + jnp.where(first_lane, side, roll_lanes(to_n, 1)) + jnp.where(last_lane, side, back(to_s, 1))
            piece = piece + roll_lanes(piece_n, 1) + back(piece_s, 1)
            results.append((main, jnp.where(inside, piece, 0.0)))
        for g, result in zip(blocks, results):
            for k in range(2):
                lh[k, g:g + SUB, :] = result[k]
        adjoint(step)

    outh_ref[...] = lh[0, own, :]


def local(checkpoint, holder_list, height, land_mask, diffusivity, tracer_weight, height_weight):
    n, n_y = lax.axis_size("gx"), lax.axis_size("gy")
    width_x, width_y = height.shape
    assert (width_x, width_y) == (SUB, LANE)
    levels = diffusivity.shape[1]
    channels = 3 * levels
    each = channels // GROUPS
    piece_rows = checkpoint.shape[3] // LANE
    padded = -(-piece_rows // SUB) * SUB
    f32 = jnp.float32
    vmem = pl.BlockSpec(memory_space=pltpu.VMEM)
    tile = pltpu.VMEM((SUB, LANE), f32)
    field = pltpu.VMEM((2, 3 * SUB, LANE), f32)
    fields = pltpu.VMEM((ITERS, 2, 3 * SUB, LANE), f32)
    volume = pltpu.VMEM((channels, 3 * SUB, LANE), f32)

    def strips(*lead):
        return pltpu.VMEM((*lead, 3 * SUB, LANE), f32)

    half = channels * HALO // SUB
    out, out_h = pl.pallas_call(
        functools.partial(kernel, n, n_y, levels, piece_rows),
        out_shape=(pltpu.VMEM((channels, SUB, LANE), f32), pltpu.VMEM((SUB, LANE), f32)),
        in_specs=[pl.BlockSpec(memory_space=pltpu.HBM)] * 7,
        out_specs=(vmem, vmem),
        scratch_shapes=[
            pltpu.VMEM((n * padded, LANE), f32),
            pltpu.VMEM((n, padded, LANE), f32),
            pltpu.VMEM((ITERS, channels, 3 * SUB, LANE), f32),
            strips(ITERS, each + 2),
            volume, strips(each),
            volume, strips(each + 2),
            pltpu.VMEM((3, channels, 3 * SUB, LANE), f32), strips(3, each),
            strips(each),
            pltpu.VMEM((each, SUB, LANE), f32),
            fields, fields, fields,
            field, field, field, field, field,
            strips(8),
            pltpu.VMEM((8, SUB, LANE), f32),
            strips(2, 8),
            pltpu.VMEM((3, each // 2, SUB, LANE), f32),
            strips(3, 2, each // 2),
            pltpu.VMEM((2, 2, half, SUB, LANE), f32),
            pltpu.VMEM((2, 2, half, SUB, LANE), f32),
            pltpu.VMEM((2, half // 2, SUB, LANE), f32),
            pltpu.VMEM((2, half // 2, SUB, LANE), f32),
            pltpu.SMEM(holder_list.shape, jnp.int32),
            pltpu.SMEM(diffusivity.shape, f32),
            pltpu.VMEM(checkpoint.shape[2:], f32),
            tile,
            pltpu.VMEM((SUB, LANE), jnp.int32),
            tile,
            pltpu.SemaphoreType.DMA((n,)),
            pltpu.SemaphoreType.DMA((n,)),
            pltpu.SemaphoreType.DMA((48,)),
            pltpu.SemaphoreType.DMA((48,)),
            pltpu.SemaphoreType.DMA((7,)),
        ],
        compiler_params=pltpu.CompilerParams(
            collective_id=0, has_side_effects=True, vmem_limit_bytes=60 * 2**20
        ),
    )(
        holder_list, diffusivity, checkpoint.reshape(checkpoint.shape[2:]), height, land_mask,
        tracer_weight.reshape(channels, SUB, LANE), height_weight,
    )
    return out.reshape(tracer_weight.shape), out_h


def solution(mesh):
    return jax.shard_map(
        local,
        mesh=mesh,
        in_specs=(
            P(("member", "gx"), "gy", None, None),
            P(("member", "gx"), "gy", None),
            P(("member", "gx"), "gy"),
            P("gx", "gy"),
            P(),
            P("member", None, "gx", "gy"),
            P(("member", "gx"), "gy"),
        ),
        out_specs=(P("member", None, "gx", "gy"), P(("member", "gx"), "gy")),
        check_vma=False,
    )
```
